32 devices in a mesh: groups: 2 (over y), gx: 4 (over z), gy: 2 (over x), gz: 2 (over core).
Axes of the slice: x: 2, y: 2, z: 4, core: 2. Of those that a mesh axis runs over, the one named last changes fastest.
Arguments:
- concentration: float32 [32, 2, 8, 128, 128], P(('groups', 'gx', 'gy', 'gz')), parts along dimension 0, may hold values from -6 to 6
- diffusivity: float32 [32, 8, 128, 128], P(('groups', 'gx', 'gy', 'gz')), parts along dimension 0, may hold values from 0.05 to 1
- rates: float32 [32, 2], P(('groups', 'gx', 'gy', 'gz')), parts along dimension 0, may hold values from 0.2 to 1.5
- velocity: float32 [4, 3], P('groups'), parts along dimension 0, may hold values from -1 to 1
- neighbours: int32 [32, 2], P('groups'), parts along dimension 0, may hold values from -1 to 15, as said below
- migrate: int32 [3, 32], P(None, 'groups'), parts along dimension 1, may hold values 0 or 1
- bit_order: int32 [6], P('groups'), parts along dimension 0, may hold values from 0 to 3, as said below
Outputs:
- final_field: float32 [32, 2, 8, 128, 128], P(('groups', 'gx', 'gy', 'gz')), parts along dimension 0
The draws below stay inside these ranges and needn't reach their ends.
There are 2 independent parts, one for each index of `groups`. The reference program is written for one: setup_inputs(seed, part) draws one part's arguments, and reference() takes and returns one part's arrays. A program takes and returns all parts, laid end to end along the dimension named above; each array names one. Nothing has to cross between parts.
Inputs may be any that keep to these rules, and one draw needn't show every extreme that they name: `neighbours`: column 0 names the patch beside a patch's first x cell, column 1 the one beside its last, -1 where the domain ends; if q is beside p on one side then p is beside q on the other. `bit_order`: distinct bit numbers of the device number within a run; the highest bit is among them.
All inputs are finite; a program needn't handle non-finite values.
Results may differ from the reference program's by a relative error of at most 0.00002.
Values sent between devices are 32-bit elements; how exact they have to be, the bound alone decides.
No kernel may reach another device: no remote copies, remote signals or barrier semaphores. Data moves between devices by JAX's collectives and lax.ppermute only.
A program may use at most 128 MiB of HBM per device.

```python
import math
import jax
import jax.numpy as jnp

PATCH_DEV = 1
PZ = 8
PY = 128
PX = 128
STEPS = 4
ROUNDS = 3
NDEV = 16
NP = 16


def draw_neighbours(key, part):
    key = jax.random.fold_in(key, 11)
    first, second = jax.random.split(key)
    total = PATCH_DEV * NDEV
    place = jnp.arange(total, dtype=jnp.int32)
    score = place * 4 + jax.random.randint(first, (total,), 0, 12)
    chain = jnp.argsort(score * total + place, stable=True).astype(jnp.int32)
    rank = jnp.argsort(chain, stable=True).astype(jnp.int32)
    links = jax.random.randint(second, (total - 1,), 0, 6) > 0
    none = jnp.full((1,), -1, jnp.int32)
    closed = jnp.zeros((1,), bool)
    chain_next = jnp.concatenate([chain[1:], none])
    chain_prev = jnp.concatenate([none, chain[:-1]])
    link_after = jnp.concatenate([links, closed])
    link_before = jnp.concatenate([closed, links])
    right = jnp.where(link_after[rank], chain_next[rank], -1)
    left = jnp.where(link_before[rank], chain_prev[rank], -1)
    return jnp.stack([left, right], axis=1).astype(jnp.int32)


def draw_bit_order(key, part):
    key = jax.random.fold_in(key, 12)
    first, second = jax.random.split(key)
    count = NDEV.bit_length() - 1
    lower = jax.random.permutation(first, count - 1).astype(jnp.int32)
    where_top = jax.random.randint(second, (), 0, ROUNDS).astype(jnp.int32)
    index = jnp.arange(ROUNDS, dtype=jnp.int32)
    before = lower[jnp.clip(index, 0, count - 2)]
    after = lower[jnp.clip(index - 1, 0, count - 2)]
    chosen = jnp.where(index < where_top, before, after)
    chosen = jnp.where(index == where_top, jnp.int32(count - 1), chosen)
    return chosen.astype(jnp.int32)


def set_ends(array, rng, smallest, high):
    spot = [jax.random.randint(jax.random.fold_in(rng, axis), (), 0, length) for axis, length in enumerate(array.shape)]
    widest = array.shape.index(max(array.shape))
    next_to = spot[:widest] + [(spot[widest] + 1) % array.shape[widest]] + spot[widest + 1:]
    return array.at[tuple(spot)].set(smallest).at[tuple(next_to)].set(high)


def steps_of(key, shape, shards, smallest, high):
    level = 1.0
    for dim, shards_of in shards:
        steps = jax.random.uniform(jax.random.fold_in(jax.random.fold_in(key, 6), dim), (shards_of,), jnp.float32, smallest / len(shards), high / len(shards))
        level = level * jnp.repeat(jnp.exp(steps), shape[dim] // shards_of).reshape((-1,) + (1,) * (len(shape) - 1 - dim))
    return level


def normal_values(key, dims, scale, most, cuts=(), kind=jnp.bfloat16):
    values = scale * jax.random.normal(key, dims, jnp.float32)
    if cuts:
        values = values * steps_of(key, dims, cuts, -0.22, 0.18)
    return jnp.clip(values, -most, most).astype(kind)


def setup_inputs(seed: int = 0, part: int = 0) -> dict:
    key_list = jax.random.split(jax.random.key(seed), 8)
    own_keys = jax.random.split(jax.random.fold_in(key_list[7], part), 8)
    concentration = normal_values(own_keys[0], (NP, 2, PZ, PY, PX), 1.0, 6.0, ((0, 16),), jnp.float32)
    diffusivity = jnp.clip(jnp.exp(math.log(1.0) - 2.9957323 * jax.random.uniform(own_keys[1], (NP, PZ, PY, PX), jnp.float32) ** steps_of(own_keys[1], (NP, PZ, PY, PX), ((0, 16),), -0.2, 0.2)), 0.05, 1.0)
    rates = jnp.clip(0.2 + 1.3 * jax.random.uniform(own_keys[2], (NP, 2), jnp.float32) ** steps_of(own_keys[2], (NP, 2), ((0, 16),), -0.2, 0.2), 0.2, 1.5)
    velocity = jnp.clip(jax.random.uniform(own_keys[3], (2, 3), jnp.float32, -1.0, 1.0), -1.0, 1.0)
    neighbours = draw_neighbours(jax.random.fold_in(jax.random.fold_in(key_list[7], part), 71), part)
    migrate = set_ends((jax.random.randint(own_keys[5], (ROUNDS, NP), 0, 3) < 1).astype(jnp.int32), jax.random.fold_in(own_keys[5], 1), 0, 1)
    bit_order = draw_bit_order(jax.random.fold_in(jax.random.fold_in(key_list[7], part), 71), part)
    return {"concentration": concentration, "diffusivity": diffusivity, "rates": rates, "velocity": velocity, "neighbours": neighbours, "migrate": migrate, "bit_order": bit_order}


time_step = 0.1


def face_flux(lower, upper, kappa_lower, kappa_upper, speed):
    return jnp.maximum(speed, 0.0) * lower + jnp.minimum(speed, 0.0) * upper - 0.5 * (kappa_lower + kappa_upper) * (upper - lower)


def advance(field, kappa, left_field, right_field, left_kappa, right_kappa, rates, velocity):
    speed_x = velocity[None, :, 0, None, None, None]
    speed_y = velocity[None, :, 1, None, None, None]
    speed_z = velocity[None, :, 2, None, None, None]
    spread = kappa[:, None]
    next_field = jnp.concatenate([field[..., 1:], right_field[..., None]], axis=-1)
    prior_field = jnp.concatenate([left_field[..., None], field[..., :-1]], axis=-1)
    next_kappa = jnp.concatenate([spread[..., 1:], right_kappa[:, None, :, :, None]], axis=-1)
    prior_kappa = jnp.concatenate([left_kappa[:, None, :, :, None], spread[..., :-1]], axis=-1)
    divergence = face_flux(field, next_field, spread, next_kappa, speed_x) - face_flux(prior_field, field, prior_kappa, spread, speed_x)
    across_y = face_flux(field[..., :-1, :], field[..., 1:, :], spread[..., :-1, :], spread[..., 1:, :], speed_y)
    divergence = divergence + jnp.pad(across_y, ((0, 0), (0, 0), (0, 0), (0, 1), (0, 0))) - jnp.pad(across_y, ((0, 0), (0, 0), (0, 0), (1, 0), (0, 0)))
    across_z = face_flux(field[:, :, :-1], field[:, :, 1:], spread[:, :, :-1], spread[:, :, 1:], speed_z)
    divergence = divergence + jnp.pad(across_z, ((0, 0), (0, 0), (0, 1), (0, 0), (0, 0))) - jnp.pad(across_z, ((0, 0), (0, 0), (1, 0), (0, 0), (0, 0)))
    first = field[:, 0]
    second = field[:, 1]
    product = rates[:, 0, None, None, None] * first * second
    reaction = jnp.stack([-product, product - rates[:, 1, None, None, None] * second], axis=1)
    return field + time_step * (reaction - divergence)


def reference(concentration, diffusivity, rates, velocity, neighbours, migrate, bit_order):
    total = concentration.shape[0]
    left_ids = neighbours[:, 0]
    right_ids = neighbours[:, 1]
    has_left = left_ids >= 0
    has_right = right_ids >= 0
    safe_left = jnp.maximum(left_ids, 0).astype(jnp.int32)
    safe_right = jnp.maximum(right_ids, 0).astype(jnp.int32)
    left_kappa = jnp.where(has_left[:, None, None], diffusivity[:, :, :, -1][safe_left], 0.0)
    right_kappa = jnp.where(has_right[:, None, None], diffusivity[:, :, :, 0][safe_right], 0.0)
    field = concentration
    for step in range(STEPS):
        left_field = jnp.where(has_left[:, None, None, None], field[:, :, :, :, -1][safe_left], 0.0)
        right_field = jnp.where(has_right[:, None, None, None], field[:, :, :, :, 0][safe_right], 0.0)
        field = advance(field, diffusivity, left_field, right_field, left_kappa, right_kappa, rates, velocity)
    slots = jnp.arange(total, dtype=jnp.int32)
    layout = slots
    for step in range(ROUNDS):
        partner = jnp.bitwise_xor(slots // PATCH_DEV, jnp.left_shift(jnp.int32(1), bit_order[step])) * PATCH_DEV + slots % PATCH_DEV
        moved = (migrate[step] + migrate[step][partner]) > 0
        layout = jnp.where(moved, layout[partner], layout)
    return field[layout]
```

```python
from functools import partial
from itertools import permutations

import jax
import jax.numpy as jnp
from jax import lax
from jax.experimental import pallas as pl
from jax.experimental.pallas import tpu as pltpu
from jax.sharding import PartitionSpec as P

time_step = 0.1
AXES = ("gx", "gy", "gz")
ROUNDS = 3
STEPS = ROUNDS + 1
LANES = 128
ROWS = 8
SMEM = pl.BlockSpec(memory_space=pltpu.SMEM)
VMEM = pl.BlockSpec(memory_space=pltpu.VMEM)
PARAMS = pltpu.CompilerParams(vmem_limit_bytes=32 * 2**20)


def lane_index():
    return lax.broadcasted_iota(jnp.int32, (ROWS, LANES), 1)


def row_index():
    return lax.broadcasted_iota(jnp.int32, (ROWS, LANES), 0)


def speeds(velocity_ref, species, direction):
    v = velocity_ref[species, direction] * time_step
    return jnp.maximum(v, 0.0), jnp.minimum(v, 0.0)


def prepare_kernel(bits, here_ref, neighbours_ref, migrate_ref, order_ref, rates_ref, u_ref, k_ref, plan_ref, own_ref, sent_ref):
    here = here_ref[0]
    for side in range(2):
        beside = neighbours_ref[here, side]
        plan_ref[side] = jnp.maximum(beside, 0)
        plan_ref[2 + side] = (beside >= 0).astype(jnp.int32)
    top = bits - 1
    order = [order_ref[r] for r in range(ROUNDS)]
    place = jnp.where(order[0] == top, 0, jnp.where(order[1] == top, 1, 2))
    first = jnp.where(place == 0, order[1], order[0])
    second = jnp.where(place == 2, order[1], order[2])
    second = jnp.where(second > first, second - 1, second)
    plan_ref[4] = (place * top + first) * (top - 1) + second
    for r in range(ROUNDS):
        partner = jnp.bitwise_xor(here, jnp.left_shift(jnp.int32(1), order[r]))
        plan_ref[5 + r] = ((migrate_ref[r, here] + migrate_ref[r, partner]) > 0).astype(jnp.int32)
    depth = k_ref.shape[0]
    wide = lax.broadcasted_iota(jnp.int32, (LANES, LANES), 1)
    for a in range(3):
        packed = jnp.zeros((LANES, LANES), jnp.float32)
        for z in range(depth):
            plane = k_ref[z] if a == 2 else u_ref[a, z]
            moved = pltpu.roll(plane, (16 * z + 8) % LANES, 1)
            packed = jnp.where((wide >= 16 * z) & (wide < 16 * z + 16), moved, packed)
        turned = packed.T
        own_ref[a] = turned.reshape(depth, 16, LANES)
        for z in range(depth):
            high = turned[16 * z : 16 * z + 8]
            low = turned[16 * z + 8 : 16 * z + 16]
            sent_ref[a * depth + z] = pltpu.roll(jnp.where(row_index() < 4, low, high), 4, 0)
    for r in range(2):
        sent_ref[3 * depth + r] = jnp.full((ROWS, LANES), rates_ref[0, r], jnp.float32)


def interior_kernel(velocity_ref, rates_ref, u_ref, k_ref, out_ref, ub, kp, kxr, kxl, ky, kz, c0):
    depth, height, _ = k_ref.shape
    blocks = height // ROWS
    half = 0.5 * time_step
    zero = jnp.zeros((ROWS, LANES), jnp.float32)
    for z in range(depth):
        for edge in (0, height + ROWS):
            kp[z, edge : edge + ROWS] = zero
            ky[z, edge : edge + ROWS] = zero
            for s in range(2):
                for i in range(2):
                    ub[s, i, z, edge : edge + ROWS] = zero
        kp[z, ROWS : ROWS + height] = k_ref[z]
        for i in range(2):
            ub[0, i, z, ROWS : ROWS + height] = u_ref[i, z]
    pos = [[speeds(velocity_ref, i, d) for d in range(3)] for i in range(2)]
    decay = time_step * rates_ref[0, 1]
    growth = time_step * rates_ref[0, 0]

    def coefficients(b, _):
        y = pl.multiple_of(b * ROWS, ROWS)
        at = y + ROWS
        row = row_index() + y
        has_next = (row < height - 1).astype(jnp.float32)
        has_prior = (row > 0).astype(jnp.float32)
        below = zero
        for z in range(depth):
            k = kp[z, pl.ds(at, ROWS)]
            xr = half * (k + pltpu.roll(k, LANES - 1, 1))
            xl = pltpu.roll(xr, 1, 1)
            yr = half * (k + kp[z, pl.ds(at + 1, ROWS)]) * has_next
            yl = half * (k + kp[z, pl.ds(at - 1, ROWS)]) * has_prior
            above = half * (k + kp[z + 1, pl.ds(at, ROWS)]) if z < depth - 1 else zero
            kxr[z, pl.ds(y, ROWS)] = xr
            kxl[z, pl.ds(y, ROWS)] = xl
            ky[z, pl.ds(at, ROWS)] = yr
            kz[z, pl.ds(y, ROWS)] = above
            total = 1.0 - ((xr + xl) + (yr + yl) + (above + below))
            for i in range(2):
                (px, mx), (py, my), (pz, mz) = pos[i]
                level = px - mx
                if z < depth - 1:
                    level = level + pz
                if z > 0:
                    level = level - mz
                if i == 1:
                    level = level + decay
                c0[i, z, pl.ds(y, ROWS)] = total - (level + py * has_next - my * has_prior)
            below = above
        return 0

    lax.fori_loop(0, blocks, coefficients, 0)

    for step in range(STEPS):
        src = step % 2

        def advance(b, _):
            y = pl.multiple_of(b * ROWS, ROWS)
            at = y + ROWS
            prior = [zero, zero]
            here = [ub[src, i, 0, pl.ds(at, ROWS)] for i in range(2)]
            zl = zero
            for z in range(depth):
                last = z == depth - 1
                after = [zero, zero] if last else [ub[src, i, z + 1, pl.ds(at, ROWS)] for i in range(2)]
                xr = kxr[z, pl.ds(y, ROWS)]
                xl = kxl[z, pl.ds(y, ROWS)]
                yr = ky[z, pl.ds(at, ROWS)]
                yl = ky[z, pl.ds(at - 1, ROWS)]
                zr = kz[z, pl.ds(y, ROWS)]
                q = (growth * here[0]) * here[1]
                for i in range(2):
                    (px, mx), (py, my), (pz, mz) = pos[i]
                    u = here[i]
                    new = c0[i, z, pl.ds(y, ROWS)] * u
                    new = new + (xr - mx) * pltpu.roll(u, LANES - 1, 1) + (xl + px) * pltpu.roll(u, 1, 1)
                    new = new + (
                        (yr - my) * ub[src, i, z, pl.ds(at + 1, ROWS)] + (yl + py) * ub[src, i, z, pl.ds(at - 1, ROWS)]
                    )
                    if not last:
                        new = new + (zr - mz) * after[i]
                    if z > 0:
                        new = new + (zl + pz) * prior[i]
                    new = new - q if i == 0 else new + q
                    if step == STEPS - 1:
                        out_ref[i, z, pl.ds(y, ROWS)] = new
                    else:
                        ub[1 - src, i, z, pl.ds(at, ROWS)] = new
                prior, here, zl = here, after, zr
            return 0

        lax.fori_loop(0, blocks, advance, 0)


def edge_kernel(plan_ref, velocity_ref, rates_ref, left_ref, right_ref, own_ref, out_ref, ub, kp, kxr, kxl, ky, kz, c0):
    depth = own_ref.shape[1]
    half = 0.5 * time_step
    zero = jnp.zeros((ROWS, LANES), jnp.float32)
    row = row_index()
    lane = lane_index()
    kept = jnp.where(row < 4, plan_ref[3], plan_ref[2]).astype(jnp.float32)

    def beside(tile):
        both = jnp.where(row < 4, left_ref[0, tile], right_ref[0, tile])
        return pltpu.roll(both, 4, 0) * kept

    decay = [jnp.full((ROWS, LANES), time_step * rates_ref[0, 1])] * 3
    growth = [jnp.full((ROWS, LANES), time_step * rates_ref[0, 0])] * 3
    growth[1] = time_step * beside(3 * depth)
    decay[1] = time_step * beside(3 * depth + 1)
    pos = [[speeds(velocity_ref, i, d) for d in range(3)] for i in range(2)]
    has_next = (lane < LANES - 1).astype(jnp.float32)
    has_prior = (lane > 0).astype(jnp.float32)
    ends = [(pos[i][1][0] * has_prior, pos[i][1][1] * has_next) for i in range(2)]
    for z in range(depth + 2):
        inside = 0 < z < depth + 1
        for block in range(5):
            at = slice(block * ROWS, block * ROWS + ROWS)
            for s in range(2):
                for i in range(2):
                    if not inside or block in (0, 4):
                        ub[s, i, z, at] = zero
            if not inside or block in (0, 4):
                kp[z, at] = zero
        if inside:
            for a in range(3):
                parts = [own_ref[a, z - 1, 0:8], beside(a * depth + z - 1), own_ref[a, z - 1, 8:16]]
                for block in range(3):
                    at = slice(block * ROWS + ROWS, block * ROWS + 2 * ROWS)
                    if a == 2:
                        kp[z, at] = parts[block]
                    else:
                        ub[0, a, z, at] = parts[block]
    for block in range(3):
        kz[0, block * ROWS : block * ROWS + ROWS] = zero

    def coefficients(z, _):
        upper = (z < depth).astype(jnp.float32)
        lower = (z > 1).astype(jnp.float32)
        for block in range(3):
            at = ROWS * (block + 1)
            here = slice(at, at + ROWS)
            put = slice(block * ROWS, block * ROWS + ROWS)
            k = kp[z, here]
            xr = half * (k + kp[z, at + 1 : at + 1 + ROWS])
            xl = half * (k + kp[z, at - 1 : at - 1 + ROWS])
            yr = half * (k + pltpu.roll(k, LANES - 1, 1)) * has_next
            yl = pltpu.roll(yr, 1, 1)
            zr = half * upper * (k + kp[z + 1, here])
            zl = half * lower * (k + kp[z - 1, here])
            kxr[z, put] = xr
            kxl[z, put] = xl
            ky[z, put] = yr
            kz[z, put] = zr
            total = 1.0 - ((xr + xl) + (yr + yl) + (zr + zl))
            for i in range(2):
                (px, mx), (py, my), (pz, mz) = pos[i]
                level = px - mx + pz * upper - mz * lower + (py * has_next - my * has_prior)
                if i == 1:
                    level = level + decay[block]
                c0[i, z, put] = total - level
        return 0

    lax.fori_loop(1, depth + 1, coefficients, 0)

    for step in range(STEPS):
        src = step % 2

        def advance(z, _):
            for block in range(3):
                at = ROWS * (block + 1)
                here = slice(at, at + ROWS)
                put = slice(block * ROWS, block * ROWS + ROWS)
                xr, xl, yr, zr, zl = kxr[z, put], kxl[z, put], ky[z, put], kz[z, put], kz[z - 1, put]
                yl = pltpu.roll(yr, 1, 1)
                pair = [ub[src, i, z, here] for i in range(2)]
                q = (growth[block] * pair[0]) * pair[1]
                for i in range(2):
                    (px, mx), _, (pz, mz) = pos[i]
                    py, my = ends[i]
                    u = pair[i]
                    new = c0[i, z, put] * u
                    new = new + (xr - mx) * ub[src, i, z, at + 1 : at + 1 + ROWS]
                    new = new + (xl + px) * ub[src, i, z, at - 1 : at - 1 + ROWS]
                    new = new + ((yr - my) * pltpu.roll(u, LANES - 1, 1) + (yl + py) * pltpu.roll(u, 1, 1))
                    new = new + ((zr - mz) * ub[src, i, z + 1, here] + (zl + pz) * ub[src, i, z - 1, here])
                    new = new - q if i == 0 else new + q
                    if block == 1:
                        new = new * kept
                    ub[1 - src, i, z, here] = new
            return 0

        lax.fori_loop(1, depth + 1, advance, 0)
    for i in range(2):
        for z in range(depth):
            high = ub[STEPS % 2, i, z + 1, ROWS : 2 * ROWS]
            low = ub[STEPS % 2, i, z + 1, 3 * ROWS : 4 * ROWS]
            out_ref[i, z] = pltpu.roll(jnp.where(row < 4, low, high), 4, 0)


def merge_kernel(u_ref, edge_ref, out_ref):
    depth = u_ref.shape[1]
    turned = edge_ref[...].reshape(2 * depth * ROWS, LANES).T
    wide = lax.broadcasted_iota(jnp.int32, (LANES, LANES), 1)
    rim = (wide < 4) | (wide >= LANES - 4)
    for i in range(2):
        for z in range(depth):
            shift = (LANES - 4 - ROWS * (i * depth + z)) % LANES
            out_ref[i, z] = jnp.where(rim, pltpu.roll(turned, shift, 1), u_ref[i, z])


def swap(block, bit):
    count = lax.axis_size(AXES)
    return lax.ppermute(block, AXES, [(low, low ^ 1 << bit) for low in range(count)])


def route(field, moved, bits, sizes):
    out = []
    start = 0
    for size in sizes:
        part = field[start : start + size]
        for r, bit in enumerate(bits):
            part = jnp.where(moved[r] > 0, swap(part, bit), part)
        out.append(part)
        start += size
    return jnp.concatenate(out, axis=0)


def per_device(concentration, diffusivity, rates, velocity, neighbours, migrate, bit_order):
    devices = lax.axis_size(AXES)
    bits = devices.bit_length() - 1
    _, species, depth, height, width = concentration.shape
    field = concentration[0]
    kappa = diffusivity[0]
    here = lax.axis_index(AXES).astype(jnp.int32).reshape(1)
    f32 = jnp.float32
    tiles = 3 * depth + 2
    plan, own, sent = pl.pallas_call(
        partial(prepare_kernel, bits),
        out_shape=(
            jax.ShapeDtypeStruct((8,), jnp.int32),
            jax.ShapeDtypeStruct((3, depth, 16, LANES), f32),
            jax.ShapeDtypeStruct((tiles, ROWS, LANES), f32),
        ),
        in_specs=[SMEM] * 5 + [VMEM] * 2,
        out_specs=(SMEM, VMEM, VMEM),
        compiler_params=PARAMS,
        name="prepare",
    )(here, neighbours, migrate, bit_order, rates, field, kappa)
    gathered = lax.all_gather(sent, AXES, axis=0, tiled=False)
    padded = height + 2 * ROWS
    inner = pl.pallas_call(
        interior_kernel,
        out_shape=jax.ShapeDtypeStruct(field.shape, f32),
        in_specs=[SMEM] * 2 + [VMEM] * 2,
        out_specs=VMEM,
        scratch_shapes=[
            pltpu.VMEM((2, species, depth, padded, width), f32),
            pltpu.VMEM((depth, padded, width), f32),
            pltpu.VMEM((depth, height, width), f32),
            pltpu.VMEM((depth, height, width), f32),
            pltpu.VMEM((depth, padded, width), f32),
            pltpu.VMEM((depth, height, width), f32),
            pltpu.VMEM((species, depth, height, width), f32),
        ],
        compiler_params=PARAMS,
        cost_estimate=pl.CostEstimate(flops=40_000_000, bytes_accessed=10_000_000, transcendentals=0),
        name="interior",
    )(velocity, rates, field, kappa)
    edges = pl.pallas_call(
        edge_kernel,
        out_shape=jax.ShapeDtypeStruct((species, depth, ROWS, LANES), f32),
        grid_spec=pltpu.PrefetchScalarGridSpec(
            num_scalar_prefetch=1,
            grid=(1,),
            in_specs=[
                SMEM,
                SMEM,
                pl.BlockSpec((1, tiles, ROWS, LANES), lambda i, plan: (plan[0], 0, 0, 0)),
                pl.BlockSpec((1, tiles, ROWS, LANES), lambda i, plan: (plan[1], 0, 0, 0)),
                VMEM,
            ],
            out_specs=pl.BlockSpec((species, depth, ROWS, LANES), lambda i, plan: (0, 0, 0, 0)),
            scratch_shapes=[
                pltpu.VMEM((2, species, depth + 2, 40, LANES), f32),
                pltpu.VMEM((depth + 2, 40, LANES), f32),
                pltpu.VMEM((depth + 2, 24, LANES), f32),
                pltpu.VMEM((depth + 2, 24, LANES), f32),
                pltpu.VMEM((depth + 2, 24, LANES), f32),
                pltpu.VMEM((depth + 2, 24, LANES), f32),
                pltpu.VMEM((species, depth + 2, 24, LANES), f32),
            ],
        ),
        compiler_params=PARAMS,
        name="edges",
    )(plan, velocity, rates, gathered, gathered, own)
    whole = pl.pallas_call(
        merge_kernel,
        out_shape=jax.ShapeDtypeStruct(field.shape, f32),
        in_specs=[VMEM] * 2,
        out_specs=VMEM,
        compiler_params=PARAMS,
        name="merge",
    )(inner, edges)
    planes = whole.reshape(species * depth, height, width)
    top = bits - 1
    branches = []
    for place in range(ROUNDS):
        for others in permutations(range(top), 2):
            order = list(others)
            order.insert(place, top)
            sizes = [(4, 4, 4, 4), (2, 4, 4, 4, 2), (2, 4, 5, 5)][place] if devices <= 16 else (species * depth,)
            if place == 0 and devices <= 16:
                sizes = (5, 5, 4, 2)
            branches.append(partial(route, bits=order, sizes=sizes))
    final = lax.switch(plan[4], branches, planes, plan[5:8])
    return final.reshape(concentration.shape)


def solution(mesh):
    spread = ("groups",) + AXES
    in_specs = (
        P(spread, None, None, None, None),
        P(spread, None, None, None),
        P(spread, None),
        P("groups", None),
        P("groups", None),
        P(None, "groups"),
        P("groups"),
    )
    out_specs = P(spread, None, None, None, None)
    return jax.shard_map(per_device, mesh=mesh, in_specs=in_specs, out_specs=out_specs, check_vma=False)
```

```python
from functools import partial
from itertools import permutations

import jax
import jax.numpy as jnp
from jax import lax
from jax.experimental import pallas as pl
from jax.experimental.pallas import tpu as pltpu
from jax.sharding import PartitionSpec as P

time_step = 0.1
AXES = ("gx", "gy", "gz")
ROUNDS = 3
STEPS = ROUNDS + 1
LANES = 128
ROWS = 8
SMEM = pl.BlockSpec(memory_space=pltpu.SMEM)
VMEM = pl.BlockSpec(memory_space=pltpu.VMEM)
PARAMS = pltpu.CompilerParams(vmem_limit_bytes=32 * 2**20)


def lane_index():
    return lax.broadcasted_iota(jnp.int32, (ROWS, LANES), 1)


def row_index():
    return lax.broadcasted_iota(jnp.int32, (ROWS, LANES), 0)


def speeds(velocity_ref, species, direction):
    v = velocity_ref[species, direction] * time_step
    return jnp.maximum(v, 0.0), jnp.minimum(v, 0.0)


def prepare_kernel(bits, here_ref, neighbours_ref, migrate_ref, order_ref, rates_ref, u_ref, k_ref, plan_ref, own_ref, sent_ref):
    here = here_ref[0]
    for side in range(2):
        beside = neighbours_ref[here, side]
        plan_ref[side] = jnp.maximum(beside, 0)
        plan_ref[2 + side] = (beside >= 0).astype(jnp.int32)
    top = bits - 1
    order = [order_ref[r] for r in range(ROUNDS)]
    place = jnp.where(order[0] == top, 0, jnp.where(order[1] == top, 1, 2))
    first = jnp.where(place == 0, order[1], order[0])
    second = jnp.where(place == 2, order[1], order[2])
    second = jnp.where(second > first, second - 1, second)
    plan_ref[4] = (place * top + first) * (top - 1) + second
    for r in range(ROUNDS):
        partner = jnp.bitwise_xor(here, jnp.left_shift(jnp.int32(1), order[r]))
        plan_ref[5 + r] = ((migrate_ref[r, here] + migrate_ref[r, partner]) > 0).astype(jnp.int32)
    depth = k_ref.shape[0]
    wide = lax.broadcasted_iota(jnp.int32, (LANES, LANES), 1)
    for a in range(3):
        packed = jnp.zeros((LANES, LANES), jnp.float32)
        for z in range(depth):
            plane = k_ref[z] if a == 2 else u_ref[a, z]
            moved = pltpu.roll(plane, (16 * z + 8) % LANES, 1)
            packed = jnp.where((wide >= 16 * z) & (wide < 16 * z + 16), moved, packed)
        turned = packed.T
        own_ref[a] = turned.reshape(depth, 16, LANES)
        for z in range(depth):
            high = turned[16 * z : 16 * z + 8]
            low = turned[16 * z + 8 : 16 * z + 16]
            sent_ref[a * depth + z] = pltpu.roll(jnp.where(row_index() < 4, low, high), 4, 0)
    for r in range(2):
        sent_ref[3 * depth + r] = jnp.full((ROWS, LANES), rates_ref[0, r], jnp.float32)


def interior_kernel(velocity_ref, rates_ref, u_ref, k_ref, out_ref, ub, kp, kxr, kxl, ky, kz, c0):
    depth, height, _ = k_ref.shape
    blocks = height // ROWS
    half = 0.5 * time_step
    zero = jnp.zeros((ROWS, LANES), jnp.float32)
    for z in range(depth):
        for edge in (0, height + ROWS):
            kp[z, edge : edge + ROWS] = zero
            ky[z, edge : edge + ROWS] = zero
            for s in range(2):
                for i in range(2):
                    ub[s, i, z, edge : edge + ROWS] = zero
        kp[z, ROWS : ROWS + height] = k_ref[z]
        for i in range(2):
            ub[0, i, z, ROWS : ROWS + height] = u_ref[i, z]
    pos = [[speeds(velocity_ref, i, d) for d in range(3)] for i in range(2)]
    decay = time_step * rates_ref[0, 1]
    growth = time_step * rates_ref[0, 0]

    def coefficients(b, _):
        y = pl.multiple_of(b * ROWS, ROWS)
        at = y + ROWS
        row = row_index() + y
        has_next = (row < height - 1).astype(jnp.float32)
        has_prior = (row > 0).astype(jnp.float32)
        below = zero
        for z in range(depth):
            k = kp[z, pl.ds(at, ROWS)]
            xr = half * (k + pltpu.roll(k, LANES - 1, 1))
            xl = pltpu.roll(xr, 1, 1)
            yr = half * (k + kp[z, pl.ds(at + 1, ROWS)]) * has_next
            yl = half * (k + kp[z, pl.ds(at - 1, ROWS)]) * has_prior
            above = half * (k + kp[z + 1, pl.ds(at, ROWS)]) if z < depth - 1 else zero
            kxr[z, pl.ds(y, ROWS)] = xr
            kxl[z, pl.ds(y, ROWS)] = xl
            ky[z, pl.ds(at, ROWS)] = yr
            kz[z, pl.ds(y, ROWS)] = above
            total = 1.0 - ((xr + xl) + (yr + yl) + (above + below))
            for i in range(2):
                (px, mx), (py, my), (pz, mz) = pos[i]
                level = px - mx
                if z < depth - 1:
                    level = level + pz
                if z > 0:
                    level = level - mz
                if i == 1:
                    level = level + decay
                c0[i, z, pl.ds(y, ROWS)] = total - (level + py * has_next - my * has_prior)
            below = above
        return 0

    lax.fori_loop(0, blocks, coefficients, 0)

    for step in range(STEPS):
        src = step % 2

        def advance(b, _):
            y = pl.multiple_of(b * ROWS, ROWS)
            at = y + ROWS
            prior = [zero, zero]
            here = [ub[src, i, 0, pl.ds(at, ROWS)] for i in range(2)]
            zl = zero
            for z in range(depth):
                last = z == depth - 1
                after = [zero, zero] if last else [ub[src, i, z + 1, pl.ds(at, ROWS)] for i in range(2)]
                xr = kxr[z, pl.ds(y, ROWS)]
                xl = kxl[z, pl.ds(y, ROWS)]
                yr = ky[z, pl.ds(at, ROWS)]
                yl = ky[z, pl.ds(at - 1, ROWS)]
                zr = kz[z, pl.ds(y, ROWS)]
                q = (growth * here[0]) * here[1]
                for i in range(2):
                    (px, mx), (py, my), (pz, mz) = pos[i]
                    u = here[i]
                    new = c0[i, z, pl.ds(y, ROWS)] * u
                    new = new + (xr - mx) * pltpu.roll(u, LANES - 1, 1) + (xl + px) * pltpu.roll(u, 1, 1)
                    new = new + (
                        (yr - my) * ub[src, i, z, pl.ds(at + 1, ROWS)] + (yl + py) * ub[src, i, z, pl.ds(at - 1, ROWS)]
                    )
                    if not last:
                        new = new + (zr - mz) * after[i]
                    if z > 0:
                        new = new + (zl + pz) * prior[i]
                    new = new - q if i == 0 else new + q
                    if step == STEPS - 1:
                        out_ref[i, z, pl.ds(y, ROWS)] = new
                    else:
                        ub[1 - src, i, z, pl.ds(at, ROWS)] = new
                prior, here, zl = here, after, zr
            return 0

        lax.fori_loop(0, blocks, advance, 0)


def edge_kernel(plan_ref, velocity_ref, rates_ref, left_ref, right_ref, own_ref, out_ref, ub, kp, kxr, kxl, ky, kz, c0):
    depth = own_ref.shape[1]
    half = 0.5 * time_step
    zero = jnp.zeros((ROWS, LANES), jnp.float32)
    row = row_index()
    lane = lane_index()
    kept = jnp.where(row < 4, plan_ref[3], plan_ref[2]).astype(jnp.float32)

    def beside(tile):
        both = jnp.where(row < 4, left_ref[0, tile], right_ref[0, tile])
        return pltpu.roll(both, 4, 0) * kept

    decay = [jnp.full((ROWS, LANES), time_step * rates_ref[0, 1])] * 3
    growth = [jnp.full((ROWS, LANES), time_step * rates_ref[0, 0])] * 3
    growth[1] = time_step * beside(3 * depth)
    decay[1] = time_step * beside(3 * depth + 1)
    pos = [[speeds(velocity_ref, i, d) for d in range(3)] for i in range(2)]
    has_next = (lane < LANES - 1).astype(jnp.float32)
    has_prior = (lane > 0).astype(jnp.float32)
    ends = [(pos[i][1][0] * has_prior, pos[i][1][1] * has_next) for i in range(2)]
    for z in range(depth + 2):
        inside = 0 < z < depth + 1
        for block in range(5):
            at = slice(block * ROWS, block * ROWS + ROWS)
            for s in range(2):
                for i in range(2):
                    if not inside or block in (0, 4):
                        ub[s, i, z, at] = zero
            if not inside or block in (0, 4):
                kp[z, at] = zero
        if inside:
            for a in range(3):
                parts = [own_ref[a, z - 1, 0:8], beside(a * depth + z - 1), own_ref[a, z - 1, 8:16]]
                for block in range(3):
                    at = slice(block * ROWS + ROWS, block * ROWS + 2 * ROWS)
                    if a == 2:
                        kp[z, at] = parts[block]
                    else:
                        ub[0, a, z, at] = parts[block]
    for block in range(3):
        kz[0, block * ROWS : block * ROWS + ROWS] = zero

    def coefficients(z, _):
        upper = (z < depth).astype(jnp.float32)
        lower = (z > 1).astype(jnp.float32)
        for block in range(3):
            at = ROWS * (block + 1)
            here = slice(at, at + ROWS)
            put = slice(block * ROWS, block * ROWS + ROWS)
            k = kp[z, here]
            xr = half * (k + kp[z, at + 1 : at + 1 + ROWS])
            xl = half * (k + kp[z, at - 1 : at - 1 + ROWS])
            yr = half * (k + pltpu.roll(k, LANES - 1, 1)) * has_next
            yl = pltpu.roll(yr, 1, 1)
            zr = half * upper * (k + kp[z + 1, here])
            zl = half * lower * (k + kp[z - 1, here])
            kxr[z, put] = xr
            kxl[z, put] = xl
            ky[z, put] = yr
            kz[z, put] = zr
            total = 1.0 - ((xr + xl) + (yr + yl) + (zr + zl))
            for i in range(2):
                (px, mx), (py, my), (pz, mz) = pos[i]
                level = px - mx + pz * upper - mz * lower + (py * has_next - my * has_prior)
                if i == 1:
                    level = level + decay[block]
                c0[i, z, put] = total - level
        return 0

    lax.fori_loop(1, depth + 1, coefficients, 0)

    for step in range(STEPS):
        src = step % 2

        def advance(z, _):
            for block in range(3):
                at = ROWS * (block + 1)
                here = slice(at, at + ROWS)
                put = slice(block * ROWS, block * ROWS + ROWS)
                xr, xl, yr, zr, zl = kxr[z, put], kxl[z, put], ky[z, put], kz[z, put], kz[z - 1, put]
                yl = pltpu.roll(yr, 1, 1)
                pair = [ub[src, i, z, here] for i in range(2)]
                q = (growth[block] * pair[0]) * pair[1]
                for i in range(2):
                    (px, mx), _, (pz, mz) = pos[i]
                    py, my = ends[i]
                    u = pair[i]
                    new = c0[i, z, put] * u
                    new = new + (xr - mx) * ub[src, i, z, at + 1 : at + 1 + ROWS]
                    new = new + (xl + px) * ub[src, i, z, at - 1 : at - 1 + ROWS]
                    new = new + ((yr - my) * pltpu.roll(u, LANES - 1, 1) + (yl + py) * pltpu.roll(u, 1, 1))
                    new = new + ((zr - mz) * ub[src, i, z + 1, here] + (zl + pz) * ub[src, i, z - 1, here])
                    new = new - q if i == 0 else new + q
                    if block == 1:
                        new = new * kept
                    ub[1 - src, i, z, here] = new
            return 0

        lax.fori_loop(1, depth + 1, advance, 0)
    for i in range(2):
        for z in range(depth):
            high = ub[STEPS % 2, i, z + 1, ROWS : 2 * ROWS]
            low = ub[STEPS % 2, i, z + 1, 3 * ROWS : 4 * ROWS]
            out_ref[i, z] = pltpu.roll(jnp.where(row < 4, low, high), 4, 0)


def merge_kernel(u_ref, edge_ref, out_ref):
    depth = u_ref.shape[1]
    turned = edge_ref[...].reshape(2 * depth * ROWS, LANES).T
    wide = lax.broadcasted_iota(jnp.int32, (LANES, LANES), 1)
    rim = (wide < 4) | (wide >= LANES - 4)
    for i in range(2):
        for z in range(depth):
            shift = (LANES - 4 - ROWS * (i * depth + z)) % LANES
            out_ref[i, z] = jnp.where(rim, pltpu.roll(turned, shift, 1), u_ref[i, z])


def swap(block, bit):
    count = lax.axis_size(AXES)
    return lax.ppermute(block, AXES, [(low, low ^ 1 << bit) for low in range(count)])


def route(field, moved, bits, sizes):
    top = max(bits)
    done = [[] for _ in bits]
    start = 0
    for size in sizes:
        part = field[start : start + size]
        for r, bit in enumerate(bits):
            ahead = 2 if bit == top else 1
            if len(done[r]) >= ahead:
                part, done[r][-ahead] = lax.optimization_barrier((part, done[r][-ahead]))
            other = swap(part, bit)
            part = jnp.where(moved[r] > 0, other, part)
            done[r].append(part)
        start += size
    return jnp.concatenate(done[-1], axis=0)


def per_device(concentration, diffusivity, rates, velocity, neighbours, migrate, bit_order):
    devices = lax.axis_size(AXES)
    bits = devices.bit_length() - 1
    _, species, depth, height, width = concentration.shape
    field = concentration[0]
    kappa = diffusivity[0]
    here = lax.axis_index(AXES).astype(jnp.int32).reshape(1)
    f32 = jnp.float32
    tiles = 3 * depth + 2
    plan, own, sent = pl.pallas_call(
        partial(prepare_kernel, bits),
        out_shape=(
            jax.ShapeDtypeStruct((8,), jnp.int32),
            jax.ShapeDtypeStruct((3, depth, 16, LANES), f32),
            jax.ShapeDtypeStruct((tiles, ROWS, LANES), f32),
        ),
        in_specs=[SMEM] * 5 + [VMEM] * 2,
        out_specs=(SMEM, VMEM, VMEM),
        compiler_params=PARAMS,
        name="prepare",
    )(here, neighbours, migrate, bit_order, rates, field, kappa)
    gathered = lax.all_gather(sent, AXES, axis=0, tiled=False)
    padded = height + 2 * ROWS
    inner = pl.pallas_call(
        interior_kernel,
        out_shape=jax.ShapeDtypeStruct(field.shape, f32),
        in_specs=[SMEM] * 2 + [VMEM] * 2,
        out_specs=VMEM,
        scratch_shapes=[
            pltpu.VMEM((2, species, depth, padded, width), f32),
            pltpu.VMEM((depth, padded, width), f32),
            pltpu.VMEM((depth, height, width), f32),
            pltpu.VMEM((depth, height, width), f32),
            pltpu.VMEM((depth, padded, width), f32),
            pltpu.VMEM((depth, height, width), f32),
            pltpu.VMEM((species, depth, height, width), f32),
        ],
        compiler_params=PARAMS,
        cost_estimate=pl.CostEstimate(flops=40_000_000, bytes_accessed=10_000_000, transcendentals=0),
        name="interior",
    )(velocity, rates, field, kappa)
    edges = pl.pallas_call(
        edge_kernel,
        out_shape=jax.ShapeDtypeStruct((species, depth, ROWS, LANES), f32),
        grid_spec=pltpu.PrefetchScalarGridSpec(
            num_scalar_prefetch=1,
            grid=(1,),
            in_specs=[
                SMEM,
                SMEM,
                pl.BlockSpec((1, tiles, ROWS, LANES), lambda i, plan: (plan[0], 0, 0, 0)),
                pl.BlockSpec((1, tiles, ROWS, LANES), lambda i, plan: (plan[1], 0, 0, 0)),
                VMEM,
            ],
            out_specs=pl.BlockSpec((species, depth, ROWS, LANES), lambda i, plan: (0, 0, 0, 0)),
            scratch_shapes=[
                pltpu.VMEM((2, species, depth + 2, 40, LANES), f32),
                pltpu.VMEM((depth + 2, 40, LANES), f32),
                pltpu.VMEM((depth + 2, 24, LANES), f32),
                pltpu.VMEM((depth + 2, 24, LANES), f32),
                pltpu.VMEM((depth + 2, 24, LANES), f32),
                pltpu.VMEM((depth + 2, 24, LANES), f32),
                pltpu.VMEM((species, depth + 2, 24, LANES), f32),
            ],
        ),
        compiler_params=PARAMS,
        name="edges",
    )(plan, velocity, rates, gathered, gathered, own)
    whole = pl.pallas_call(
        merge_kernel,
        out_shape=jax.ShapeDtypeStruct(field.shape, f32),
        in_specs=[VMEM] * 2,
        out_specs=VMEM,
        compiler_params=PARAMS,
        name="merge",
    )(inner, edges)
    planes = whole.reshape(species * depth, height, width)
    top = bits - 1
    branches = []
    for place in range(ROUNDS):
        for others in permutations(range(top), 2):
            order = list(others)
            order.insert(place, top)
            sizes = (2,) * depth if devices <= 16 else (species * depth,)
            branches.append(partial(route, bits=order, sizes=sizes))
    final = lax.switch(plan[4], branches, planes, plan[5:8])
    return final.reshape(concentration.shape)


def solution(mesh):
    spread = ("groups",) + AXES
    in_specs = (
        P(spread, None, None, None, None),
        P(spread, None, None, None),
        P(spread, None),
        P("groups", None),
        P("groups", None),
        P(None, "groups"),
        P("groups"),
    )
    out_specs = P(spread, None, None, None, None)
    return jax.shard_map(per_device, mesh=mesh, in_specs=in_specs, out_specs=out_specs, check_vma=False)
```

```python
from functools import partial
from itertools import combinations

import jax
import jax.numpy as jnp
from jax import lax
from jax.experimental import pallas as pl
from jax.experimental.pallas import tpu as pltpu
from jax.sharding import PartitionSpec as P

time_step = 0.1
AXES = ("gx", "gy", "gz")
ROUNDS = 3
STEPS = ROUNDS + 1
LANES = 128
ROWS = 8
SMEM = pl.BlockSpec(memory_space=pltpu.SMEM)
VMEM = pl.BlockSpec(memory_space=pltpu.VMEM)
PARAMS = pltpu.CompilerParams(vmem_limit_bytes=32 * 2**20)


def lane_index():
    return lax.broadcasted_iota(jnp.int32, (ROWS, LANES), 1)


def row_index():
    return lax.broadcasted_iota(jnp.int32, (ROWS, LANES), 0)


def speeds(velocity_ref, species, direction):
    v = velocity_ref[species, direction] * time_step
    return jnp.maximum(v, 0.0), jnp.minimum(v, 0.0)


def prepare_kernel(top, here_ref, neighbours_ref, migrate_ref, order_ref, rates_ref, u_ref, k_ref, plan_ref, own_ref, sent_ref):
    here = here_ref[0]
    for side in range(2):
        beside = neighbours_ref[here, side]
        plan_ref[side] = jnp.maximum(beside, 0)
        plan_ref[2 + side] = (beside >= 0).astype(jnp.int32)
    order = [order_ref[r] for r in range(ROUNDS)]
    low = jnp.minimum(jnp.minimum(order[0], order[1]), order[2])
    high = order[0] + order[1] + order[2] - top - low
    plan_ref[4] = ((low * (2 * top - 1 - low)) >> 1) + high - low - 1

    def source(slot):
        for r in reversed(range(ROUNDS)):
            partner = jnp.bitwise_xor(slot, jnp.left_shift(jnp.int32(1), order[r]))
            slot = jnp.where(migrate_ref[r, slot] + migrate_ref[r, partner] > 0, partner, slot)
        return slot

    def candidate(slot):
        apart = jnp.bitwise_xor(source(slot), here)
        return ((apart >> top) & 1) + 2 * ((apart >> low) & 1), (apart >> high) & 1

    plan_ref[5], _ = candidate(jnp.bitwise_xor(here, jnp.left_shift(jnp.int32(1), high)))
    plan_ref[6], plan_ref[7] = candidate(here)
    depth = k_ref.shape[0]
    wide = lax.broadcasted_iota(jnp.int32, (LANES, LANES), 1)
    for a in range(3):
        packed = jnp.zeros((LANES, LANES), jnp.float32)
        for z in range(depth):
            plane = k_ref[z] if a == 2 else u_ref[a, z]
            moved = pltpu.roll(plane, (16 * z + 8) % LANES, 1)
            packed = jnp.where((wide >= 16 * z) & (wide < 16 * z + 16), moved, packed)
        turned = packed.T
        own_ref[a] = turned.reshape(depth, 16, LANES)
        for z in range(depth):
            high = turned[16 * z : 16 * z + 8]
            low = turned[16 * z + 8 : 16 * z + 16]
            sent_ref[a * depth + z] = pltpu.roll(jnp.where(row_index() < 4, low, high), 4, 0)
    for r in range(2):
        sent_ref[3 * depth + r] = jnp.full((ROWS, LANES), rates_ref[0, r], jnp.float32)


def interior_kernel(velocity_ref, rates_ref, u_ref, k_ref, out_ref, ub, kp, kxr, kxl, ky, kz, c0):
    depth, height, _ = k_ref.shape
    blocks = height // ROWS
    half = 0.5 * time_step
    zero = jnp.zeros((ROWS, LANES), jnp.float32)
    for z in range(depth):
        for edge in (0, height + ROWS):
            kp[z, edge : edge + ROWS] = zero
            ky[z, edge : edge + ROWS] = zero
            for s in range(2):
                for i in range(2):
                    ub[s, i, z, edge : edge + ROWS] = zero
        kp[z, ROWS : ROWS + height] = k_ref[z]
        for i in range(2):
            ub[0, i, z, ROWS : ROWS + height] = u_ref[i, z]
    pos = [[speeds(velocity_ref, i, d) for d in range(3)] for i in range(2)]
    decay = time_step * rates_ref[0, 1]
    growth = time_step * rates_ref[0, 0]

    def coefficients(b, _):
        y = pl.multiple_of(b * ROWS, ROWS)
        at = y + ROWS
        row = row_index() + y
        has_next = (row < height - 1).astype(jnp.float32)
        has_prior = (row > 0).astype(jnp.float32)
        below = zero
        for z in range(depth):
            k = kp[z, pl.ds(at, ROWS)]
            xr = half * (k + pltpu.roll(k, LANES - 1, 1))
            xl = pltpu.roll(xr, 1, 1)
            yr = half * (k + kp[z, pl.ds(at + 1, ROWS)]) * has_next
            yl = half * (k + kp[z, pl.ds(at - 1, ROWS)]) * has_prior
            above = half * (k + kp[z + 1, pl.ds(at, ROWS)]) if z < depth - 1 else zero
            kxr[z, pl.ds(y, ROWS)] = xr
            kxl[z, pl.ds(y, ROWS)] = xl
            ky[z, pl.ds(at, ROWS)] = yr
            kz[z, pl.ds(y, ROWS)] = above
            total = 1.0 - ((xr + xl) + (yr + yl) + (above + below))
            for i in range(2):
                (px, mx), (py, my), (pz, mz) = pos[i]
                level = px - mx
                if z < depth - 1:
                    level = level + pz
                if z > 0:
                    level = level - mz
                if i == 1:
                    level = level + decay
                c0[i, z, pl.ds(y, ROWS)] = total - (level + py * has_next - my * has_prior)
            below = above
        return 0

    lax.fori_loop(0, blocks, coefficients, 0)

    for step in range(STEPS):
        src = step % 2

        def advance(b, _):
            y = pl.multiple_of(b * ROWS, ROWS)
            at = y + ROWS
            prior = [zero, zero]
            here = [ub[src, i, 0, pl.ds(at, ROWS)] for i in range(2)]
            zl = zero
            for z in range(depth):
                last = z == depth - 1
                after = [zero, zero] if last else [ub[src, i, z + 1, pl.ds(at, ROWS)] for i in range(2)]
                xr = kxr[z, pl.ds(y, ROWS)]
                xl = kxl[z, pl.ds(y, ROWS)]
                yr = ky[z, pl.ds(at, ROWS)]
                yl = ky[z, pl.ds(at - 1, ROWS)]
                zr = kz[z, pl.ds(y, ROWS)]
                q = (growth * here[0]) * here[1]
                for i in range(2):
                    (px, mx), (py, my), (pz, mz) = pos[i]
                    u = here[i]
                    new = c0[i, z, pl.ds(y, ROWS)] * u
                    new = new + (xr - mx) * pltpu.roll(u, LANES - 1, 1) + (xl + px) * pltpu.roll(u, 1, 1)
                    new = new + (
                        (yr - my) * ub[src, i, z, pl.ds(at + 1, ROWS)] + (yl + py) * ub[src, i, z, pl.ds(at - 1, ROWS)]
                    )
                    if not last:
                        new = new + (zr - mz) * after[i]
                    if z > 0:
                        new = new + (zl + pz) * prior[i]
                    new = new - q if i == 0 else new + q
                    if step == STEPS - 1:
                        out_ref[i, z, pl.ds(y, ROWS)] = new
                    else:
                        ub[1 - src, i, z, pl.ds(at, ROWS)] = new
                prior, here, zl = here, after, zr
            return 0

        lax.fori_loop(0, blocks, advance, 0)


def edge_kernel(plan_ref, velocity_ref, rates_ref, left_ref, right_ref, own_ref, out_ref, ub, kp, kxr, kxl, ky, kz, c0):
    depth = own_ref.shape[1]
    half = 0.5 * time_step
    zero = jnp.zeros((ROWS, LANES), jnp.float32)
    row = row_index()
    lane = lane_index()
    kept = jnp.where(row < 4, plan_ref[3], plan_ref[2]).astype(jnp.float32)

    def beside(tile):
        both = jnp.where(row < 4, left_ref[0, tile], right_ref[0, tile])
        return pltpu.roll(both, 4, 0) * kept

    decay = [jnp.full((ROWS, LANES), time_step * rates_ref[0, 1])] * 3
    growth = [jnp.full((ROWS, LANES), time_step * rates_ref[0, 0])] * 3
    growth[1] = time_step * beside(3 * depth)
    decay[1] = time_step * beside(3 * depth + 1)
    pos = [[speeds(velocity_ref, i, d) for d in range(3)] for i in range(2)]
    has_next = (lane < LANES - 1).astype(jnp.float32)
    has_prior = (lane > 0).astype(jnp.float32)
    ends = [(pos[i][1][0] * has_prior, pos[i][1][1] * has_next) for i in range(2)]
    for z in range(depth + 2):
        inside = 0 < z < depth + 1
        for block in range(5):
            at = slice(block * ROWS, block * ROWS + ROWS)
            for s in range(2):
                for i in range(2):
                    if not inside or block in (0, 4):
                        ub[s, i, z, at] = zero
            if not inside or block in (0, 4):
                kp[z, at] = zero
        if inside:
            for a in range(3):
                parts = [own_ref[a, z - 1, 0:8], beside(a * depth + z - 1), own_ref[a, z - 1, 8:16]]
                for block in range(3):
                    at = slice(block * ROWS + ROWS, block * ROWS + 2 * ROWS)
                    if a == 2:
                        kp[z, at] = parts[block]
                    else:
                        ub[0, a, z, at] = parts[block]
    for block in range(3):
        kz[0, block * ROWS : block * ROWS + ROWS] = zero

    def coefficients(z, _):
        upper = (z < depth).astype(jnp.float32)
        lower = (z > 1).astype(jnp.float32)
        for block in range(3):
            at = ROWS * (block + 1)
            here = slice(at, at + ROWS)
            put = slice(block * ROWS, block * ROWS + ROWS)
            k = kp[z, here]
            xr = half * (k + kp[z, at + 1 : at + 1 + ROWS])
            xl = half * (k + kp[z, at - 1 : at - 1 + ROWS])
            yr = half * (k + pltpu.roll(k, LANES - 1, 1)) * has_next
            yl = pltpu.roll(yr, 1, 1)
            zr = half * upper * (k + kp[z + 1, here])
            zl = half * lower * (k + kp[z - 1, here])
            kxr[z, put] = xr
            kxl[z, put] = xl
            ky[z, put] = yr
            kz[z, put] = zr
            total = 1.0 - ((xr + xl) + (yr + yl) + (zr + zl))
            for i in range(2):
                (px, mx), (py, my), (pz, mz) = pos[i]
                level = px - mx + pz * upper - mz * lower + (py * has_next - my * has_prior)
                if i == 1:
                    level = level + decay[block]
                c0[i, z, put] = total - level
        return 0

    lax.fori_loop(1, depth + 1, coefficients, 0)

    for step in range(STEPS):
        src = step % 2

        def advance(z, _):
            for block in range(3):
                at = ROWS * (block + 1)
                here = slice(at, at + ROWS)
                put = slice(block * ROWS, block * ROWS + ROWS)
                xr, xl, yr, zr, zl = kxr[z, put], kxl[z, put], ky[z, put], kz[z, put], kz[z - 1, put]
                yl = pltpu.roll(yr, 1, 1)
                pair = [ub[src, i, z, here] for i in range(2)]
                q = (growth[block] * pair[0]) * pair[1]
                for i in range(2):
                    (px, mx), _, (pz, mz) = pos[i]
                    py, my = ends[i]
                    u = pair[i]
                    new = c0[i, z, put] * u
                    new = new + (xr - mx) * ub[src, i, z, at + 1 : at + 1 + ROWS]
                    new = new + (xl + px) * ub[src, i, z, at - 1 : at - 1 + ROWS]
                    new = new + ((yr - my) * pltpu.roll(u, LANES - 1, 1) + (yl + py) * pltpu.roll(u, 1, 1))
                    new = new + ((zr - mz) * ub[src, i, z + 1, here] + (zl + pz) * ub[src, i, z - 1, here])
                    new = new - q if i == 0 else new + q
                    if block == 1:
                        new = new * kept
                    ub[1 - src, i, z, here] = new
            return 0

        lax.fori_loop(1, depth + 1, advance, 0)
    for i in range(2):
        for z in range(depth):
            high = ub[STEPS % 2, i, z + 1, ROWS : 2 * ROWS]
            low = ub[STEPS % 2, i, z + 1, 3 * ROWS : 4 * ROWS]
            out_ref[i, z] = pltpu.roll(jnp.where(row < 4, low, high), 4, 0)


def merge_kernel(u_ref, edge_ref, out_ref):
    depth = u_ref.shape[1]
    turned = edge_ref[...].reshape(2 * depth * ROWS, LANES).T
    wide = lax.broadcasted_iota(jnp.int32, (LANES, LANES), 1)
    rim = (wide < 4) | (wide >= LANES - 4)
    for i in range(2):
        for z in range(depth):
            shift = (LANES - 4 - ROWS * (i * depth + z)) % LANES
            out_ref[i, z] = jnp.where(rim, pltpu.roll(turned, shift, 1), u_ref[i, z])


def swap(block, bit):
    count = lax.axis_size(AXES)
    return lax.ppermute(block, AXES, [(low, low ^ 1 << bit) for low in range(count)])


def pick(index, options):
    picked = options[0]
    for number in range(1, 4):
        picked = jnp.where(index == number, options[number], picked)
    return picked


def after(value, earlier):
    return lax.optimization_barrier((value, earlier))


def edge_call(plan, velocity, rates, gathered, own, tiles):
    f32 = jnp.float32
    species = 2
    depth = own.shape[1]
    return pl.pallas_call(
        edge_kernel,
        out_shape=jax.ShapeDtypeStruct((species, depth, ROWS, LANES), f32),
        grid_spec=pltpu.PrefetchScalarGridSpec(
            num_scalar_prefetch=1,
            grid=(1,),
            in_specs=[
                SMEM,
                SMEM,
                pl.BlockSpec((1, tiles, ROWS, LANES), lambda i, plan: (plan[0], 0, 0, 0)),
                pl.BlockSpec((1, tiles, ROWS, LANES), lambda i, plan: (plan[1], 0, 0, 0)),
                VMEM,
            ],
            out_specs=pl.BlockSpec((species, depth, ROWS, LANES), lambda i, plan: (0, 0, 0, 0)),
            scratch_shapes=[
                pltpu.VMEM((2, species, depth + 2, 40, LANES), f32),
                pltpu.VMEM((depth + 2, 40, LANES), f32),
                pltpu.VMEM((depth + 2, 24, LANES), f32),
                pltpu.VMEM((depth + 2, 24, LANES), f32),
                pltpu.VMEM((depth + 2, 24, LANES), f32),
                pltpu.VMEM((depth + 2, 24, LANES), f32),
                pltpu.VMEM((species, depth + 2, 24, LANES), f32),
            ],
        ),
        compiler_params=PARAMS,
        name="edges",
    )(plan, velocity, rates, gathered, gathered, own)


def spans(total):
    sizes = (5, 5, 4, 2) if total == 16 else (total,)
    return [(sum(sizes[:n]), sum(sizes[: n + 1])) for n in range(len(sizes))]


def run(low, high, top, field, kappa, rates, velocity, plan, own, sent):
    species, depth, height, width = field.shape
    f32 = jnp.float32
    tiles = sent.shape[0]
    gathered = lax.all_gather(sent, AXES, axis=0, tiled=False)
    padded = height + 2 * ROWS
    inner = pl.pallas_call(
        interior_kernel,
        out_shape=jax.ShapeDtypeStruct(field.shape, f32),
        in_specs=[SMEM] * 2 + [VMEM] * 2,
        out_specs=VMEM,
        scratch_shapes=[
            pltpu.VMEM((2, species, depth, padded, width), f32),
            pltpu.VMEM((depth, padded, width), f32),
            pltpu.VMEM((depth, height, width), f32),
            pltpu.VMEM((depth, height, width), f32),
            pltpu.VMEM((depth, padded, width), f32),
            pltpu.VMEM((depth, height, width), f32),
            pltpu.VMEM((species, depth, height, width), f32),
        ],
        compiler_params=PARAMS,
        cost_estimate=pl.CostEstimate(flops=40_000_000, bytes_accessed=10_000_000, transcendentals=0),
        name="interior",
    )(velocity, rates, field, kappa)
    planes = inner.reshape(species * depth, height, width)
    cuts = spans(species * depth)
    last = len(cuts) - 1
    across = swap(planes, low)
    near = []
    far = []
    sent_on = []
    out = []

    def start_near(n):
        part = planes[cuts[n][0] : cuts[n][1]]
        if n >= 2:
            part, near[n - 2] = after(part, near[n - 2])
        if n >= 3:
            part, far[n - 3] = after(part, far[n - 3])
        near.append(swap(part, top))

    for n in range(min(2, last + 1)):
        start_near(n)
    for n, (start, stop) in enumerate(cuts):
        part = near[n]
        if n == last:
            own, part = after(own, part) if n == 0 else (own, part)
            if n > 0:
                own, near[n - 1] = after(own, near[n - 1])
            edges = edge_call(plan, velocity, rates, gathered, own, tiles)
            part, edges = after(part, edges)
        if n >= 2:
            part, sent_on[n - 2] = after(part, sent_on[n - 2])
        far.append(swap(part, low))
        if n + 2 <= last:
            start_near(n + 2)
        options = (planes[start:stop], near[n], across[start:stop], far[n])
        sent_on.append(swap(pick(plan[5], options), high))
        out.append(jnp.where(plan[7] > 0, sent_on[n], pick(plan[6], options)))
    rim_near = swap(edges, top)
    options = (edges, rim_near, swap(edges, low), swap(rim_near, low))
    other = swap(pick(plan[5], options), high)
    rim = jnp.where(plan[7] > 0, other, pick(plan[6], options))
    final = jnp.concatenate(out, axis=0).reshape(field.shape)
    return pl.pallas_call(
        merge_kernel,
        out_shape=jax.ShapeDtypeStruct(field.shape, f32),
        in_specs=[VMEM] * 2,
        out_specs=VMEM,
        compiler_params=PARAMS,
        name="merge",
    )(final, rim)


def per_device(concentration, diffusivity, rates, velocity, neighbours, migrate, bit_order):
    top = lax.axis_size(AXES).bit_length() - 2
    field = concentration[0]
    kappa = diffusivity[0]
    depth = kappa.shape[0]
    here = lax.axis_index(AXES).astype(jnp.int32).reshape(1)
    plan, own, sent = pl.pallas_call(
        partial(prepare_kernel, top),
        out_shape=(
            jax.ShapeDtypeStruct((8,), jnp.int32),
            jax.ShapeDtypeStruct((3, depth, 16, LANES), jnp.float32),
            jax.ShapeDtypeStruct((3 * depth + 2, ROWS, LANES), jnp.float32),
        ),
        in_specs=[SMEM] * 5 + [VMEM] * 2,
        out_specs=(SMEM, VMEM, VMEM),
        compiler_params=PARAMS,
        name="prepare",
    )(here, neighbours, migrate, bit_order, rates, field, kappa)
    branches = [partial(run, low, high, top) for low, high in combinations(range(top), 2)]
    final = lax.switch(plan[4], branches, field, kappa, rates, velocity, plan, own, sent)
    return final.reshape(concentration.shape)


def solution(mesh):
    spread = ("groups",) + AXES
    in_specs = (
        P(spread, None, None, None, None),
        P(spread, None, None, None),
        P(spread, None),
        P("groups", None),
        P("groups", None),
        P(None, "groups"),
        P("groups"),
    )
    out_specs = P(spread, None, None, None, None)
    return jax.shard_map(per_device, mesh=mesh, in_specs=in_specs, out_specs=out_specs, check_vma=False)
```

```python
from functools import partial
from itertools import combinations

import jax
import jax.numpy as jnp
from jax import lax
from jax.experimental import pallas as pl
from jax.experimental.pallas import tpu as pltpu
from jax.sharding import PartitionSpec as P

time_step = 0.1
AXES = ("gx", "gy", "gz")
ROUNDS = 3
STEPS = ROUNDS + 1
LANES = 128
ROWS = 8
SMEM = pl.BlockSpec(memory_space=pltpu.SMEM)
VMEM = pl.BlockSpec(memory_space=pltpu.VMEM)
PARAMS = pltpu.CompilerParams(vmem_limit_bytes=32 * 2**20)


def lane_index():
    return lax.broadcasted_iota(jnp.int32, (ROWS, LANES), 1)


def row_index():
    return lax.broadcasted_iota(jnp.int32, (ROWS, LANES), 0)


def speeds(velocity_ref, species, direction):
    v = velocity_ref[species, direction] * time_step
    return jnp.maximum(v, 0.0), jnp.minimum(v, 0.0)


def prepare_kernel(top, here_ref, neighbours_ref, migrate_ref, order_ref, rates_ref, u_ref, k_ref, plan_ref, own_ref, sent_ref):
    here = here_ref[0]
    for side in range(2):
        beside = neighbours_ref[here, side]
        apart = jnp.bitwise_xor(jnp.maximum(beside, 0), here)
        spot = jnp.int32(0)
        for bit in range(top + 1):
            spot = spot | (((apart >> bit) & 1) << (top - bit))
        plan_ref[side] = spot
        plan_ref[2 + side] = (beside >= 0).astype(jnp.int32)
    order = [order_ref[r] for r in range(ROUNDS)]
    low = jnp.minimum(jnp.minimum(order[0], order[1]), order[2])
    high = order[0] + order[1] + order[2] - top - low
    plan_ref[4] = ((low * (2 * top - 1 - low)) >> 1) + high - low - 1

    def source(slot):
        for r in reversed(range(ROUNDS)):
            partner = jnp.bitwise_xor(slot, jnp.left_shift(jnp.int32(1), order[r]))
            slot = jnp.where(migrate_ref[r, slot] + migrate_ref[r, partner] > 0, partner, slot)
        return slot

    def candidate(slot):
        apart = jnp.bitwise_xor(source(slot), here)
        return ((apart >> top) & 1) + 2 * ((apart >> low) & 1), (apart >> high) & 1

    plan_ref[5], _ = candidate(jnp.bitwise_xor(here, jnp.left_shift(jnp.int32(1), high)))
    plan_ref[6], plan_ref[7] = candidate(here)
    depth = k_ref.shape[0]
    wide = lax.broadcasted_iota(jnp.int32, (LANES, LANES), 1)
    for a in range(3):
        packed = jnp.zeros((LANES, LANES), jnp.float32)
        for z in range(depth):
            plane = k_ref[z] if a == 2 else u_ref[a, z]
            moved = pltpu.roll(plane, (16 * z + 8) % LANES, 1)
            packed = jnp.where((wide >= 16 * z) & (wide < 16 * z + 16), moved, packed)
        turned = packed.T
        own_ref[a] = turned.reshape(depth, 16, LANES)
        for z in range(depth):
            high = turned[16 * z : 16 * z + 8]
            low = turned[16 * z + 8 : 16 * z + 16]
            sent_ref[a * depth + z] = pltpu.roll(jnp.where(row_index() < 4, low, high), 4, 0)
    for r in range(2):
        sent_ref[3 * depth + r] = jnp.full((ROWS, LANES), rates_ref[0, r], jnp.float32)


def interior_kernel(first, cuts, velocity_ref, rates_ref, u_ref, k_ref, *refs):
    out_refs, (ub, kp, kxr, kxl, ky, kz, c0) = refs[: len(cuts)], refs[len(cuts) :]
    depth, height, _ = k_ref.shape
    blocks = height // ROWS
    last = first + sum(cuts)
    start, stop = max(first - 1, 0), min(last + 1, blocks)
    half = 0.5 * time_step
    zero = jnp.zeros((ROWS, LANES), jnp.float32)
    low, high = max(start - 1, 0) * ROWS, min(stop + 1, blocks) * ROWS
    for z in range(depth):
        for edge in (0, height + ROWS):
            kp[z, edge : edge + ROWS] = zero
            ky[z, edge : edge + ROWS] = zero
            for s in range(2):
                for i in range(2):
                    ub[s, i, z, edge : edge + ROWS] = zero
        kp[z, ROWS + low : ROWS + high] = k_ref[z, low:high]
        for i in range(2):
            ub[0, i, z, ROWS + low : ROWS + high] = u_ref[i, z, low:high]
    pos = [[speeds(velocity_ref, i, d) for d in range(3)] for i in range(2)]
    decay = time_step * rates_ref[0, 1]
    growth = time_step * rates_ref[0, 0]

    def coefficients(b, _):
        y = pl.multiple_of(b * ROWS, ROWS)
        at = y + ROWS
        row = row_index() + y
        has_next = (row < height - 1).astype(jnp.float32)
        has_prior = (row > 0).astype(jnp.float32)
        below = zero
        for z in range(depth):
            k = kp[z, pl.ds(at, ROWS)]
            xr = half * (k + pltpu.roll(k, LANES - 1, 1))
            xl = pltpu.roll(xr, 1, 1)
            yr = half * (k + kp[z, pl.ds(at + 1, ROWS)]) * has_next
            yl = half * (k + kp[z, pl.ds(at - 1, ROWS)]) * has_prior
            above = half * (k + kp[z + 1, pl.ds(at, ROWS)]) if z < depth - 1 else zero
            kxr[z, pl.ds(y, ROWS)] = xr
            kxl[z, pl.ds(y, ROWS)] = xl
            ky[z, pl.ds(at, ROWS)] = yr
            kz[z, pl.ds(y, ROWS)] = above
            total = 1.0 - ((xr + xl) + (yr + yl) + (above + below))
            for i in range(2):
                (px, mx), (py, my), (pz, mz) = pos[i]
                level = px - mx
                if z < depth - 1:
                    level = level + pz
                if z > 0:
                    level = level - mz
                if i == 1:
                    level = level + decay
                c0[i, z, pl.ds(y, ROWS)] = total - (level + py * has_next - my * has_prior)
            below = above
        return 0

    lax.fori_loop(start, stop, coefficients, 0)

    def advance(src, put, b, _):
        y = pl.multiple_of(b * ROWS, ROWS)
        at = y + ROWS
        prior = [zero, zero]
        here = [ub[src, i, 0, pl.ds(at, ROWS)] for i in range(2)]
        zl = zero
        for z in range(depth):
            end = z == depth - 1
            after = [zero, zero] if end else [ub[src, i, z + 1, pl.ds(at, ROWS)] for i in range(2)]
            xr = kxr[z, pl.ds(y, ROWS)]
            xl = kxl[z, pl.ds(y, ROWS)]
            yr = ky[z, pl.ds(at, ROWS)]
            yl = ky[z, pl.ds(at - 1, ROWS)]
            zr = kz[z, pl.ds(y, ROWS)]
            q = (growth * here[0]) * here[1]
            for i in range(2):
                (px, mx), (py, my), (pz, mz) = pos[i]
                u = here[i]
                new = c0[i, z, pl.ds(y, ROWS)] * u
                new = new + (xr - mx) * pltpu.roll(u, LANES - 1, 1) + (xl + px) * pltpu.roll(u, 1, 1)
                new = new + (
                    (yr - my) * ub[src, i, z, pl.ds(at + 1, ROWS)] + (yl + py) * ub[src, i, z, pl.ds(at - 1, ROWS)]
                )
                if not end:
                    new = new + (zr - mz) * after[i]
                if z > 0:
                    new = new + (zl + pz) * prior[i]
                put(b, i, z, new - q if i == 0 else new + q)
            prior, here, zl = here, after, zr
        return 0

    for step in range(STEPS - 1):

        def keep(b, i, z, new, step=step):
            ub[1 - step % 2, i, z, pl.ds(pl.multiple_of(b * ROWS + ROWS, ROWS), ROWS)] = new

        lax.fori_loop(start, stop, partial(advance, step % 2, keep), 0)
    begin = first
    for cut, out_ref in zip(cuts, out_refs):

        def give(b, i, z, new, out_ref=out_ref, begin=begin):
            out_ref[i, z, pl.ds(pl.multiple_of((b - begin) * ROWS, ROWS), ROWS)] = new

        lax.fori_loop(begin, begin + cut, partial(advance, (STEPS - 1) % 2, give), 0)
        begin += cut


def edge_kernel(plan_ref, velocity_ref, rates_ref, left_ref, right_ref, own_ref, out_ref, ub, kp, kxr, kxl, ky, kz, c0):
    depth = own_ref.shape[1]
    half = 0.5 * time_step
    zero = jnp.zeros((ROWS, LANES), jnp.float32)
    row = row_index()
    lane = lane_index()
    kept = jnp.where(row < 4, plan_ref[3], plan_ref[2]).astype(jnp.float32)

    def beside(tile):
        both = jnp.where(row < 4, left_ref[0, tile], right_ref[0, tile])
        return pltpu.roll(both, 4, 0) * kept

    decay = [jnp.full((ROWS, LANES), time_step * rates_ref[0, 1])] * 3
    growth = [jnp.full((ROWS, LANES), time_step * rates_ref[0, 0])] * 3
    growth[1] = time_step * beside(3 * depth)
    decay[1] = time_step * beside(3 * depth + 1)
    pos = [[speeds(velocity_ref, i, d) for d in range(3)] for i in range(2)]
    has_next = (lane < LANES - 1).astype(jnp.float32)
    has_prior = (lane > 0).astype(jnp.float32)
    ends = [(pos[i][1][0] * has_prior, pos[i][1][1] * has_next) for i in range(2)]
    for z in range(depth + 2):
        inside = 0 < z < depth + 1
        for block in range(5):
            at = slice(block * ROWS, block * ROWS + ROWS)
            for s in range(2):
                for i in range(2):
                    if not inside or block in (0, 4):
                        ub[s, i, z, at] = zero
            if not inside or block in (0, 4):
                kp[z, at] = zero
        if inside:
            for a in range(3):
                parts = [own_ref[a, z - 1, 0:8], beside(a * depth + z - 1), own_ref[a, z - 1, 8:16]]
                for block in range(3):
                    at = slice(block * ROWS + ROWS, block * ROWS + 2 * ROWS)
                    if a == 2:
                        kp[z, at] = parts[block]
                    else:
                        ub[0, a, z, at] = parts[block]
    for block in range(3):
        kz[0, block * ROWS : block * ROWS + ROWS] = zero

    def coefficients(z, _):
        upper = (z < depth).astype(jnp.float32)
        lower = (z > 1).astype(jnp.float32)
        for block in range(3):
            at = ROWS * (block + 1)
            here = slice(at, at + ROWS)
            put = slice(block * ROWS, block * ROWS + ROWS)
            k = kp[z, here]
            xr = half * (k + kp[z, at + 1 : at + 1 + ROWS])
            xl = half * (k + kp[z, at - 1 : at - 1 + ROWS])
            yr = half * (k + pltpu.roll(k, LANES - 1, 1)) * has_next
            yl = pltpu.roll(yr, 1, 1)
            zr = half * upper * (k + kp[z + 1, here])
            zl = half * lower * (k + kp[z - 1, here])
            kxr[z, put] = xr
            kxl[z, put] = xl
            ky[z, put] = yr
            kz[z, put] = zr
            total = 1.0 - ((xr + xl) + (yr + yl) + (zr + zl))
            for i in range(2):
                (px, mx), (py, my), (pz, mz) = pos[i]
                level = px - mx + pz * upper - mz * lower + (py * has_next - my * has_prior)
                if i == 1:
                    level = level + decay[block]
                c0[i, z, put] = total - level
        return 0

    lax.fori_loop(1, depth + 1, coefficients, 0)

    for step in range(STEPS):
        src = step % 2

        def advance(z, _):
            for block in range(3):
                at = ROWS * (block + 1)
                here = slice(at, at + ROWS)
                put = slice(block * ROWS, block * ROWS + ROWS)
                xr, xl, yr, zr, zl = kxr[z, put], kxl[z, put], ky[z, put], kz[z, put], kz[z - 1, put]
                yl = pltpu.roll(yr, 1, 1)
                pair = [ub[src, i, z, here] for i in range(2)]
                q = (growth[block] * pair[0]) * pair[1]
                for i in range(2):
                    (px, mx), _, (pz, mz) = pos[i]
                    py, my = ends[i]
                    u = pair[i]
                    new = c0[i, z, put] * u
                    new = new + (xr - mx) * ub[src, i, z, at + 1 : at + 1 + ROWS]
                    new = new + (xl + px) * ub[src, i, z, at - 1 : at - 1 + ROWS]
                    new = new + ((yr - my) * pltpu.roll(u, LANES - 1, 1) + (yl + py) * pltpu.roll(u, 1, 1))
                    new = new + ((zr - mz) * ub[src, i, z + 1, here] + (zl + pz) * ub[src, i, z - 1, here])
                    new = new - q if i == 0 else new + q
                    if block == 1:
                        new = new * kept
                    ub[1 - src, i, z, here] = new
            return 0

        lax.fori_loop(1, depth + 1, advance, 0)
    for i in range(2):
        for z in range(depth):
            high = ub[STEPS % 2, i, z + 1, ROWS : 2 * ROWS]
            low = ub[STEPS % 2, i, z + 1, 3 * ROWS : 4 * ROWS]
            out_ref[i, z] = pltpu.roll(jnp.where(row < 4, low, high), 4, 0)


def merge_kernel(*refs):
    *part_refs, edge_ref, out_ref = refs
    depth = out_ref.shape[1]
    turned = edge_ref[...].reshape(2 * depth * ROWS, LANES).T
    begin = 0
    for part_ref in part_refs:
        rows = part_ref.shape[2]
        wide = lax.broadcasted_iota(jnp.int32, (rows, LANES), 1)
        rim = (wide < 4) | (wide >= LANES - 4)
        for i in range(2):
            for z in range(depth):
                shift = (LANES - 4 - ROWS * (i * depth + z)) % LANES
                turn = pltpu.roll(turned[begin : begin + rows], shift, 1)
                out_ref[i, z, begin : begin + rows] = jnp.where(rim, turn, part_ref[i, z])
        begin += rows


def swap(block, bit):
    count = lax.axis_size(AXES)
    return lax.ppermute(block, AXES, [(low, low ^ 1 << bit) for low in range(count)])


def pick(index, options):
    picked = options[0]
    for number in range(1, 4):
        picked = jnp.where(index == number, options[number], picked)
    return picked


def order(*values):
    return lax.optimization_barrier(values)


def interior_call(first, cuts, velocity, rates, field, kappa):
    species, depth, height, width = field.shape
    f32 = jnp.float32
    padded = height + 2 * ROWS
    return pl.pallas_call(
        partial(interior_kernel, first, cuts),
        out_shape=[jax.ShapeDtypeStruct((species, depth, cut * ROWS, width), f32) for cut in cuts],
        in_specs=[SMEM] * 2 + [VMEM] * 2,
        out_specs=[VMEM] * len(cuts),
        scratch_shapes=[
            pltpu.VMEM((2, species, depth, padded, width), f32),
            pltpu.VMEM((depth, padded, width), f32),
            pltpu.VMEM((depth, height, width), f32),
            pltpu.VMEM((depth, height, width), f32),
            pltpu.VMEM((depth, padded, width), f32),
            pltpu.VMEM((depth, height, width), f32),
            pltpu.VMEM((species, depth, height, width), f32),
        ],
        compiler_params=PARAMS,
        cost_estimate=pl.CostEstimate(flops=40_000_000, bytes_accessed=10_000_000, transcendentals=0),
        name="interior",
    )(velocity, rates, field, kappa)


def edge_call(plan, velocity, rates, gathered, own):
    f32 = jnp.float32
    species = 2
    depth = own.shape[1]
    tiles = gathered.shape[1]
    return pl.pallas_call(
        edge_kernel,
        out_shape=jax.ShapeDtypeStruct((species, depth, ROWS, LANES), f32),
        grid_spec=pltpu.PrefetchScalarGridSpec(
            num_scalar_prefetch=1,
            grid=(1,),
            in_specs=[
                SMEM,
                SMEM,
                pl.BlockSpec((1, tiles, ROWS, LANES), lambda i, plan: (plan[0], 0, 0, 0)),
                pl.BlockSpec((1, tiles, ROWS, LANES), lambda i, plan: (plan[1], 0, 0, 0)),
                VMEM,
            ],
            out_specs=pl.BlockSpec((species, depth, ROWS, LANES), lambda i, plan: (0, 0, 0, 0)),
            scratch_shapes=[
                pltpu.VMEM((2, species, depth + 2, 40, LANES), f32),
                pltpu.VMEM((depth + 2, 40, LANES), f32),
                pltpu.VMEM((depth + 2, 24, LANES), f32),
                pltpu.VMEM((depth + 2, 24, LANES), f32),
                pltpu.VMEM((depth + 2, 24, LANES), f32),
                pltpu.VMEM((depth + 2, 24, LANES), f32),
                pltpu.VMEM((species, depth + 2, 24, LANES), f32),
            ],
        ),
        compiler_params=PARAMS,
        name="edges",
    )(plan, velocity, rates, gathered, gathered, own)


def double(strips, bit):
    return jnp.concatenate([strips, swap(strips, bit)], axis=0)


def run(low, high, top, field, kappa, rates, velocity, plan, own, sent):
    blocks = field.shape[2] // ROWS
    cuts = (blocks * 7 // 16, blocks // 4, blocks * 3 // 16, blocks // 8)
    give = partial(pick, plan[5])
    keep = partial(pick, plan[6])

    def result(options, other):
        return jnp.where(plan[7] > 0, other, keep(options))

    strips = double(sent[None], top)
    (p0,) = interior_call(0, cuts[:1], velocity, rates, field, kappa)
    p0, strips, field = order(p0, strips, field)
    n0, a0 = swap(p0, top), swap(p0, low)
    p1, p2, p3 = interior_call(cuts[0], cuts[1:], velocity, rates, field, kappa)
    for bit in reversed(range(1, top)):
        strips = double(strips, bit)
        p1, strips = order(p1, strips)
    p1, p2, p3, n0, a0, strips = order(p1, p2, p3, n0, a0, strips)
    n1, a1, f0 = swap(p1, top), swap(p1, low), swap(n0, low)
    strips = double(strips, 0)
    p2, n1, a1, f0, strips = order(p2, n1, a1, f0, strips)
    o0 = (p0, n0, a0, f0)
    n2, a2, f1, h0 = swap(p2, top), swap(p2, low), swap(n1, low), swap(give(o0), high)
    edges = edge_call(plan, velocity, rates, strips, own)
    p3, n2, a2, f1, h0, edges = order(p3, n2, a2, f1, h0, edges)
    o1 = (p1, n1, a1, f1)
    n3, a3, f2, h1 = swap(p3, top), swap(p3, low), swap(n2, low), swap(give(o1), high)
    en, ea = swap(edges, top), swap(edges, low)
    n3, a3, f2, h1, en, ea = order(n3, a3, f2, h1, en, ea)
    o2 = (p2, n2, a2, f2)
    f3, h2, ef = swap(n3, low), swap(give(o2), high), swap(en, low)
    f3, h2, ef = order(f3, h2, ef)
    o3 = (p3, n3, a3, f3)
    oe = (edges, en, ea, ef)
    h3, eh = swap(give(o3), high), swap(give(oe), high)
    parts = [result(*pair) for pair in ((o0, h0), (o1, h1), (o2, h2), (o3, h3), (oe, eh))]
    return pl.pallas_call(
        merge_kernel,
        out_shape=jax.ShapeDtypeStruct(field.shape, jnp.float32),
        in_specs=[VMEM] * 5,
        out_specs=VMEM,
        compiler_params=PARAMS,
        name="merge",
    )(*parts)


def per_device(concentration, diffusivity, rates, velocity, neighbours, migrate, bit_order):
    top = lax.axis_size(AXES).bit_length() - 2
    field = concentration[0]
    kappa = diffusivity[0]
    depth = kappa.shape[0]
    here = lax.axis_index(AXES).astype(jnp.int32).reshape(1)
    plan, own, sent = pl.pallas_call(
        partial(prepare_kernel, top),
        out_shape=(
            jax.ShapeDtypeStruct((8,), jnp.int32),
            jax.ShapeDtypeStruct((3, depth, 16, LANES), jnp.float32),
            jax.ShapeDtypeStruct((3 * depth + 2, ROWS, LANES), jnp.float32),
        ),
        in_specs=[SMEM] * 5 + [VMEM] * 2,
        out_specs=(SMEM, VMEM, VMEM),
        compiler_params=PARAMS,
        name="prepare",
    )(here, neighbours, migrate, bit_order, rates, field, kappa)
    branches = [partial(run, low, high, top) for low, high in combinations(range(top), 2)]
    final = lax.switch(plan[4], branches, field, kappa, rates, velocity, plan, own, sent)
    return final.reshape(concentration.shape)


def solution(mesh):
    spread = ("groups",) + AXES
    in_specs = (
        P(spread, None, None, None, None),
        P(spread, None, None, None),
        P(spread, None),
        P("groups", None),
        P("groups", None),
        P(None, "groups"),
        P("groups"),
    )
    out_specs = P(spread, None, None, None, None)
    return jax.shard_map(per_device, mesh=mesh, in_specs=in_specs, out_specs=out_specs, check_vma=False)
```

```python
from functools import partial
from itertools import combinations

import jax
import jax.numpy as jnp
from jax import lax
from jax.experimental import pallas as pl
from jax.experimental.pallas import tpu as pltpu
from jax.sharding import PartitionSpec as P

time_step = 0.1
AXES = ("gx", "gy", "gz")
ROUNDS = 3
STEPS = ROUNDS + 1
LANES = 128
ROWS = 8
SMEM = pl.BlockSpec(memory_space=pltpu.SMEM)
VMEM = pl.BlockSpec(memory_space=pltpu.VMEM)
PARAMS = pltpu.CompilerParams(vmem_limit_bytes=32 * 2**20)


def lane_index():
    return lax.broadcasted_iota(jnp.int32, (ROWS, LANES), 1)


def row_index():
    return lax.broadcasted_iota(jnp.int32, (ROWS, LANES), 0)


def speeds(velocity_ref, species, direction):
    v = velocity_ref[species, direction] * time_step
    return jnp.maximum(v, 0.0), jnp.minimum(v, 0.0)


def prepare_kernel(
    top,
    here_ref,
    neighbours_hbm,
    migrate_hbm,
    order_hbm,
    rates_hbm,
    u_hbm,
    k_hbm,
    branch_ref,
    plan_ref,
    own_ref,
    sent_ref,
    neighbours_ref,
    migrate_ref,
    order_ref,
    rates_ref,
    u_ref,
    k_ref,
    sems,
):
    pairs = (
        (neighbours_hbm, neighbours_ref),
        (migrate_hbm, migrate_ref),
        (order_hbm, order_ref),
        (rates_hbm, rates_ref),
        (u_hbm, u_ref),
        (k_hbm, k_ref),
    )
    copies = [pltpu.make_async_copy(src, dst, sems.at[n]) for n, (src, dst) in enumerate(pairs)]
    for copy in copies:
        copy.start()
    for copy in copies:
        copy.wait()
    here = here_ref[0]
    for side in range(2):
        beside = neighbours_ref[side, here]
        plan_ref[side] = jnp.bitwise_xor(jnp.maximum(beside, 0), here)
        plan_ref[2 + side] = (beside >= 0).astype(jnp.int32)
    order = [order_ref[r] for r in range(ROUNDS)]
    low = jnp.minimum(jnp.minimum(order[0], order[1]), order[2])
    high = order[0] + order[1] + order[2] - top - low
    branch_ref[0] = ((low * (2 * top - 1 - low)) >> 1) + high - low - 1

    def source(slot):
        for r in reversed(range(ROUNDS)):
            partner = jnp.bitwise_xor(slot, jnp.left_shift(jnp.int32(1), order[r]))
            slot = jnp.where(migrate_ref[r, slot] + migrate_ref[r, partner] > 0, partner, slot)
        return slot

    def candidate(slot):
        apart = jnp.bitwise_xor(source(slot), here)
        return ((apart >> top) & 1) + 2 * ((apart >> low) & 1), (apart >> high) & 1

    plan_ref[5], _ = candidate(jnp.bitwise_xor(here, jnp.left_shift(jnp.int32(1), high)))
    plan_ref[6], plan_ref[7] = candidate(here)
    depth = k_ref.shape[0]
    wide = lax.broadcasted_iota(jnp.int32, (LANES, LANES), 1)
    for a in range(3):
        packed = jnp.zeros((LANES, LANES), jnp.float32)
        for z in range(depth):
            plane = k_ref[z] if a == 2 else u_ref[a, z]
            moved = pltpu.roll(plane, (16 * z + 8) % LANES, 1)
            packed = jnp.where((wide >= 16 * z) & (wide < 16 * z + 16), moved, packed)
        turned = packed.T
        own_ref[a] = turned.reshape(depth, 16, LANES)
        for z in range(depth):
            high = turned[16 * z : 16 * z + 8]
            low = turned[16 * z + 8 : 16 * z + 16]
            sent_ref[a * depth + z] = pltpu.roll(jnp.where(row_index() < 4, low, high), 4, 0)
    for r in range(2):
        sent_ref[3 * depth + r] = jnp.full((ROWS, LANES), rates_ref[0, r], jnp.float32)


def interior_kernel(first, cuts, velocity_ref, rates_ref, u_ref, k_ref, *refs):
    out_refs, (ub, kp, kxr, kxl, ky, kz, c0) = refs[: len(cuts)], refs[len(cuts) :]
    depth, height, _ = k_ref.shape
    blocks = height // ROWS
    last = first + sum(cuts)
    start, stop = max(first - 1, 0), min(last + 1, blocks)
    half = 0.5 * time_step
    zero = jnp.zeros((ROWS, LANES), jnp.float32)
    low, high = max(start - 1, 0) * ROWS, min(stop + 1, blocks) * ROWS
    for z in range(depth):
        for edge in (0, height + ROWS):
            kp[z, edge : edge + ROWS] = zero
            ky[z, edge : edge + ROWS] = zero
            for s in range(2):
                for i in range(2):
                    ub[s, i, z, edge : edge + ROWS] = zero
        kp[z, ROWS + low : ROWS + high] = k_ref[z, low:high]
        for i in range(2):
            ub[0, i, z, ROWS + low : ROWS + high] = u_ref[i, z, low:high]
    pos = [[speeds(velocity_ref, i, d) for d in range(3)] for i in range(2)]
    decay = time_step * rates_ref[0, 1]
    growth = time_step * rates_ref[0, 0]

    def coefficients(b, _):
        y = pl.multiple_of(b * ROWS, ROWS)
        at = y + ROWS
        row = row_index() + y
        has_next = (row < height - 1).astype(jnp.float32)
        has_prior = (row > 0).astype(jnp.float32)
        below = zero
        for z in range(depth):
            k = kp[z, pl.ds(at, ROWS)]
            xr = half * (k + pltpu.roll(k, LANES - 1, 1))
            xl = pltpu.roll(xr, 1, 1)
            yr = half * (k + kp[z, pl.ds(at + 1, ROWS)]) * has_next
            yl = half * (k + kp[z, pl.ds(at - 1, ROWS)]) * has_prior
            above = half * (k + kp[z + 1, pl.ds(at, ROWS)]) if z < depth - 1 else zero
            kxr[z, pl.ds(y, ROWS)] = xr
            kxl[z, pl.ds(y, ROWS)] = xl
            ky[z, pl.ds(at, ROWS)] = yr
            kz[z, pl.ds(y, ROWS)] = above
            total = 1.0 - ((xr + xl) + (yr + yl) + (above + below))
            for i in range(2):
                (px, mx), (py, my), (pz, mz) = pos[i]
                level = px - mx
                if z < depth - 1:
                    level = level + pz
                if z > 0:
                    level = level - mz
                if i == 1:
                    level = level + decay
                c0[i, z, pl.ds(y, ROWS)] = total - (level + py * has_next - my * has_prior)
            below = above
        return 0

    lax.fori_loop(start, stop, coefficients, 0)

    def advance(src, put, b, _):
        y = pl.multiple_of(b * ROWS, ROWS)
        at = y + ROWS
        prior = [zero, zero]
        here = [ub[src, i, 0, pl.ds(at, ROWS)] for i in range(2)]
        zl = zero
        for z in range(depth):
            end = z == depth - 1
            after = [zero, zero] if end else [ub[src, i, z + 1, pl.ds(at, ROWS)] for i in range(2)]
            xr = kxr[z, pl.ds(y, ROWS)]
            xl = kxl[z, pl.ds(y, ROWS)]
            yr = ky[z, pl.ds(at, ROWS)]
            yl = ky[z, pl.ds(at - 1, ROWS)]
            zr = kz[z, pl.ds(y, ROWS)]
            q = (growth * here[0]) * here[1]
            for i in range(2):
                (px, mx), (py, my), (pz, mz) = pos[i]
                u = here[i]
                new = c0[i, z, pl.ds(y, ROWS)] * u
                new = new + (xr - mx) * pltpu.roll(u, LANES - 1, 1) + (xl + px) * pltpu.roll(u, 1, 1)
                new = new + (
                    (yr - my) * ub[src, i, z, pl.ds(at + 1, ROWS)] + (yl + py) * ub[src, i, z, pl.ds(at - 1, ROWS)]
                )
                if not end:
                    new = new + (zr - mz) * after[i]
                if z > 0:
                    new = new + (zl + pz) * prior[i]
                put(b, i, z, new - q if i == 0 else new + q)
            prior, here, zl = here, after, zr
        return 0

    for step in range(STEPS - 1):

        def keep(b, i, z, new, step=step):
            ub[1 - step % 2, i, z, pl.ds(pl.multiple_of(b * ROWS + ROWS, ROWS), ROWS)] = new

        lax.fori_loop(start, stop, partial(advance, step % 2, keep), 0)
    begin = first
    for cut, out_ref in zip(cuts, out_refs):

        def give(b, i, z, new, out_ref=out_ref, begin=begin):
            out_ref[i, z, pl.ds(pl.multiple_of((b - begin) * ROWS, ROWS), ROWS)] = new

        lax.fori_loop(begin, begin + cut, partial(advance, (STEPS - 1) % 2, give), 0)
        begin += cut


def edge_kernel(plan_ref, velocity_ref, rates_ref, left_ref, right_ref, own_ref, out_ref, ub, kp, kxr, kxl, ky, kz, c0):
    depth = own_ref.shape[1]
    half = 0.5 * time_step
    zero = jnp.zeros((ROWS, LANES), jnp.float32)
    row = row_index()
    lane = lane_index()
    kept = jnp.where(row < 4, plan_ref[3], plan_ref[2]).astype(jnp.float32)

    def beside(tile):
        both = jnp.where(row < 4, left_ref[0, tile], right_ref[0, tile])
        return pltpu.roll(both, 4, 0) * kept

    decay = [jnp.full((ROWS, LANES), time_step * rates_ref[0, 1])] * 3
    growth = [jnp.full((ROWS, LANES), time_step * rates_ref[0, 0])] * 3
    growth[1] = time_step * beside(3 * depth)
    decay[1] = time_step * beside(3 * depth + 1)
    pos = [[speeds(velocity_ref, i, d) for d in range(3)] for i in range(2)]
    has_next = (lane < LANES - 1).astype(jnp.float32)
    has_prior = (lane > 0).astype(jnp.float32)
    ends = [(pos[i][1][0] * has_prior, pos[i][1][1] * has_next) for i in range(2)]
    for z in range(depth + 2):
        inside = 0 < z < depth + 1
        for block in range(5):
            at = slice(block * ROWS, block * ROWS + ROWS)
            for s in range(2):
                for i in range(2):
                    if not inside or block in (0, 4):
                        ub[s, i, z, at] = zero
            if not inside or block in (0, 4):
                kp[z, at] = zero
        if inside:
            for a in range(3):
                parts = [own_ref[a, z - 1, 0:8], beside(a * depth + z - 1), own_ref[a, z - 1, 8:16]]
                for block in range(3):
                    at = slice(block * ROWS + ROWS, block * ROWS + 2 * ROWS)
                    if a == 2:
                        kp[z, at] = parts[block]
                    else:
                        ub[0, a, z, at] = parts[block]
    for block in range(3):
        kz[0, block * ROWS : block * ROWS + ROWS] = zero

    def coefficients(z, _):
        upper = (z < depth).astype(jnp.float32)
        lower = (z > 1).astype(jnp.float32)
        for block in range(3):
            at = ROWS * (block + 1)
            here = slice(at, at + ROWS)
            put = slice(block * ROWS, block * ROWS + ROWS)
            k = kp[z, here]
            xr = half * (k + kp[z, at + 1 : at + 1 + ROWS])
            xl = half * (k + kp[z, at - 1 : at - 1 + ROWS])
            yr = half * (k + pltpu.roll(k, LANES - 1, 1)) * has_next
            yl = pltpu.roll(yr, 1, 1)
            zr = half * upper * (k + kp[z + 1, here])
            zl = half * lower * (k + kp[z - 1, here])
            kxr[z, put] = xr
            kxl[z, put] = xl
            ky[z, put] = yr
            kz[z, put] = zr
            total = 1.0 - ((xr + xl) + (yr + yl) + (zr + zl))
            for i in range(2):
                (px, mx), (py, my), (pz, mz) = pos[i]
                level = px - mx + pz * upper - mz * lower + (py * has_next - my * has_prior)
                if i == 1:
                    level = level + decay[block]
                c0[i, z, put] = total - level
        return 0

    lax.fori_loop(1, depth + 1, coefficients, 0)

    for step in range(STEPS):
        src = step % 2

        def advance(z, _):
            for block in range(3):
                at = ROWS * (block + 1)
                here = slice(at, at + ROWS)
                put = slice(block * ROWS, block * ROWS + ROWS)
                xr, xl, yr, zr, zl = kxr[z, put], kxl[z, put], ky[z, put], kz[z, put], kz[z - 1, put]
                yl = pltpu.roll(yr, 1, 1)
                pair = [ub[src, i, z, here] for i in range(2)]
                q = (growth[block] * pair[0]) * pair[1]
                for i in range(2):
                    (px, mx), _, (pz, mz) = pos[i]
                    py, my = ends[i]
                    u = pair[i]
                    new = c0[i, z, put] * u
                    new = new + (xr - mx) * ub[src, i, z, at + 1 : at + 1 + ROWS]
                    new = new + (xl + px) * ub[src, i, z, at - 1 : at - 1 + ROWS]
                    new = new + ((yr - my) * pltpu.roll(u, LANES - 1, 1) + (yl + py) * pltpu.roll(u, 1, 1))
                    new = new + ((zr - mz) * ub[src, i, z + 1, here] + (zl + pz) * ub[src, i, z - 1, here])
                    new = new - q if i == 0 else new + q
                    if block == 1:
                        new = new * kept
                    ub[1 - src, i, z, here] = new
            return 0

        lax.fori_loop(1, depth + 1, advance, 0)
    for i in range(2):
        for z in range(depth):
            high = ub[STEPS % 2, i, z + 1, ROWS : 2 * ROWS]
            low = ub[STEPS % 2, i, z + 1, 3 * ROWS : 4 * ROWS]
            out_ref[i, z] = pltpu.roll(jnp.where(row < 4, low, high), 4, 0)


def merge_kernel(*refs):
    *part_refs, edge_ref, out_ref = refs
    depth = out_ref.shape[1]
    turned = edge_ref[...].reshape(2 * depth * ROWS, LANES).T
    begin = 0
    for part_ref in part_refs:
        rows = part_ref.shape[2]
        wide = lax.broadcasted_iota(jnp.int32, (rows, LANES), 1)
        rim = (wide < 4) | (wide >= LANES - 4)
        for i in range(2):
            for z in range(depth):
                shift = (LANES - 4 - ROWS * (i * depth + z)) % LANES
                turn = pltpu.roll(turned[begin : begin + rows], shift, 1)
                out_ref[i, z, begin : begin + rows] = jnp.where(rim, turn, part_ref[i, z])
        begin += rows


def swap_mask(block, mask):
    return lax.ppermute(block, AXES, [(slot, slot ^ mask) for slot in range(lax.axis_size(AXES))])


def swap(block, bit):
    return swap_mask(block, 1 << bit)


def swap_both(block, first, second):
    return swap_mask(block, 1 << first | 1 << second)


def pick(index, options):
    picked = options[0]
    for number in range(1, 4):
        picked = jnp.where(index == number, options[number], picked)
    return picked


def order(*values):
    return lax.optimization_barrier(values)


def interior_call(first, cuts, velocity, rates, field, kappa):
    species, depth, height, width = field.shape
    f32 = jnp.float32
    padded = height + 2 * ROWS
    return pl.pallas_call(
        partial(interior_kernel, first, cuts),
        out_shape=[jax.ShapeDtypeStruct((species, depth, cut * ROWS, width), f32) for cut in cuts],
        in_specs=[SMEM] * 2 + [VMEM] * 2,
        out_specs=[VMEM] * len(cuts),
        scratch_shapes=[
            pltpu.VMEM((2, species, depth, padded, width), f32),
            pltpu.VMEM((depth, padded, width), f32),
            pltpu.VMEM((depth, height, width), f32),
            pltpu.VMEM((depth, height, width), f32),
            pltpu.VMEM((depth, padded, width), f32),
            pltpu.VMEM((depth, height, width), f32),
            pltpu.VMEM((species, depth, height, width), f32),
        ],
        compiler_params=PARAMS,
        cost_estimate=pl.CostEstimate(flops=40_000_000, bytes_accessed=10_000_000, transcendentals=0),
        name="interior",
    )(velocity, rates, field, kappa)


def edge_call(plan, velocity, rates, gathered, own, bits):
    f32 = jnp.float32
    species = 2
    depth = own.shape[1]
    tiles = gathered.shape[1]

    def spot(apart):
        place = 0
        for n, bit in enumerate(bits):
            place = place | (((apart >> bit) & 1) << n)
        return place

    return pl.pallas_call(
        edge_kernel,
        out_shape=jax.ShapeDtypeStruct((species, depth, ROWS, LANES), f32),
        grid_spec=pltpu.PrefetchScalarGridSpec(
            num_scalar_prefetch=1,
            grid=(1,),
            in_specs=[
                SMEM,
                SMEM,
                pl.BlockSpec((1, tiles, ROWS, LANES), lambda i, plan: (spot(plan[0]), 0, 0, 0)),
                pl.BlockSpec((1, tiles, ROWS, LANES), lambda i, plan: (spot(plan[1]), 0, 0, 0)),
                VMEM,
            ],
            out_specs=pl.BlockSpec((species, depth, ROWS, LANES), lambda i, plan: (0, 0, 0, 0)),
            scratch_shapes=[
                pltpu.VMEM((2, species, depth + 2, 40, LANES), f32),
                pltpu.VMEM((depth + 2, 40, LANES), f32),
                pltpu.VMEM((depth + 2, 24, LANES), f32),
                pltpu.VMEM((depth + 2, 24, LANES), f32),
                pltpu.VMEM((depth + 2, 24, LANES), f32),
                pltpu.VMEM((depth + 2, 24, LANES), f32),
                pltpu.VMEM((species, depth + 2, 24, LANES), f32),
            ],
        ),
        compiler_params=PARAMS,
        name="edges",
    )(plan, velocity, rates, gathered, gathered, own)


def double(strips, bit):
    return jnp.concatenate([strips, swap(strips, bit)], axis=0)


def run(low, high, top, field, kappa, rates, velocity, plan, own, sent):
    blocks = field.shape[2] // ROWS
    cuts = (blocks // 4,) * 4
    middle = [bit for bit in reversed(range(1, top)) if bit != low]
    if low:
        middle.insert(0, low)
    give = partial(pick, plan[5])
    keep = partial(pick, plan[6])

    def result(options, other):
        return jnp.where(plan[7] > 0, other, keep(options))

    strips = double(sent[None], top)
    (p0,) = interior_call(0, cuts[:1], velocity, rates, field, kappa)
    p0, strips, field = order(p0, strips, field)
    n0, a0 = swap(p0, top), swap(p0, low)
    strips = double(strips, middle[0])
    p1, p2, p3 = interior_call(cuts[0], cuts[1:], velocity, rates, field, kappa)
    p1, p2, p3, n0, a0, strips = order(p1, p2, p3, n0, a0, strips)
    n1, a1, f0 = swap(p1, top), swap(p1, low), swap(n0, low)
    for bit in middle[1:]:
        strips = double(strips, bit)
    p2, n1, a1, f0, strips = order(p2, n1, a1, f0, strips)
    o0 = (p0, n0, a0, f0)
    n2, a2, f1, h0 = swap(p2, top), swap(p2, low), swap(n1, low), swap(give(o0), high)
    strips = double(strips, 0)
    p3, n2, a2, f1, h0, strips = order(p3, n2, a2, f1, h0, strips)
    o1 = (p1, n1, a1, f1)
    n3, a3, f2, h1 = swap(p3, top), swap(p3, low), swap(n2, low), swap(give(o1), high)
    edges = edge_call(plan, velocity, rates, strips, own, [top, *middle, 0])
    n3, a3, f2, h1, edges = order(n3, a3, f2, h1, edges)
    o2 = (p2, n2, a2, f2)
    f3, h2 = swap(n3, low), swap(give(o2), high)
    oe = (edges, swap(edges, top), swap(edges, low), swap_both(edges, top, low))
    f3, h2, *oe = order(f3, h2, *oe)
    o3 = (p3, n3, a3, f3)
    h3, eh = swap(give(o3), high), swap(give(oe), high)
    parts = [result(*pair) for pair in ((o0, h0), (o1, h1), (o2, h2), (o3, h3), (oe, eh))]
    return pl.pallas_call(
        merge_kernel,
        out_shape=jax.ShapeDtypeStruct(field.shape, jnp.float32),
        in_specs=[VMEM] * 5,
        out_specs=VMEM,
        compiler_params=PARAMS,
        name="merge",
    )(*parts)


def per_device(concentration, diffusivity, rates, velocity, neighbours, migrate, bit_order):
    top = lax.axis_size(AXES).bit_length() - 2
    field = concentration[0]
    kappa = diffusivity[0]
    depth = kappa.shape[0]
    here = lax.axis_index(AXES).astype(jnp.int32).reshape(1)
    branch, plan, own, sent = pl.pallas_call(
        partial(prepare_kernel, top),
        out_shape=(
            jax.ShapeDtypeStruct((1,), jnp.int32),
            jax.ShapeDtypeStruct((8,), jnp.int32),
            jax.ShapeDtypeStruct((3, depth, 16, LANES), jnp.float32),
            jax.ShapeDtypeStruct((3 * depth + 2, ROWS, LANES), jnp.float32),
        ),
        in_specs=[SMEM] + [pl.BlockSpec(memory_space=pl.ANY)] * 6,
        out_specs=(SMEM, SMEM, VMEM, VMEM),
        scratch_shapes=[
            pltpu.SMEM(neighbours.shape[::-1], jnp.int32),
            pltpu.SMEM(migrate.shape, jnp.int32),
            pltpu.SMEM(bit_order.shape, jnp.int32),
            pltpu.SMEM(rates.shape, jnp.float32),
            pltpu.VMEM(field.shape, jnp.float32),
            pltpu.VMEM(kappa.shape, jnp.float32),
            pltpu.SemaphoreType.DMA((6,)),
        ],
        compiler_params=pltpu.CompilerParams(vmem_limit_bytes=60 * 2**20),
        name="prepare",
    )(here, neighbours.T, migrate, bit_order, rates, field, kappa)
    branches = [partial(run, low, high, top) for low, high in combinations(range(top), 2)]
    final = lax.switch(branch[0], branches, field, kappa, rates, velocity, plan, own, sent)
    return final.reshape(concentration.shape)


def solution(mesh):
    spread = ("groups",) + AXES
    in_specs = (
        P(spread, None, None, None, None),
        P(spread, None, None, None),
        P(spread, None),
        P("groups", None),
        P("groups", None),
        P(None, "groups"),
        P("groups"),
    )
    out_specs = P(spread, None, None, None, None)
    return jax.shard_map(per_device, mesh=mesh, in_specs=in_specs, out_specs=out_specs, check_vma=False)
```

```python
from functools import partial
from itertools import combinations

import jax
import jax.numpy as jnp
from jax import lax
from jax.experimental import pallas as pl
from jax.experimental.pallas import tpu as pltpu
from jax.sharding import PartitionSpec as P

time_step = 0.1
AXES = ("gx", "gy", "gz")
ROUNDS = 3
STEPS = ROUNDS + 1
LANES = 128
ROWS = 8
SMEM = pl.BlockSpec(memory_space=pltpu.SMEM)
VMEM = pl.BlockSpec(memory_space=pltpu.VMEM)
PARAMS = pltpu.CompilerParams(vmem_limit_bytes=32 * 2**20)


def lane_index():
    return lax.broadcasted_iota(jnp.int32, (ROWS, LANES), 1)


def row_index():
    return lax.broadcasted_iota(jnp.int32, (ROWS, LANES), 0)


def speeds(velocity_ref, species, direction):
    v = velocity_ref[species, direction] * time_step
    return jnp.maximum(v, 0.0), jnp.minimum(v, 0.0)


def prepare_kernel(
    top,
    here_ref,
    neighbours_hbm,
    migrate_hbm,
    order_hbm,
    rates_hbm,
    u_hbm,
    k_hbm,
    branch_ref,
    plan_ref,
    own_ref,
    sent_ref,
    neighbours_ref,
    migrate_ref,
    order_ref,
    rates_ref,
    u_ref,
    k_ref,
    sems,
):
    pairs = (
        (neighbours_hbm, neighbours_ref),
        (migrate_hbm, migrate_ref),
        (order_hbm, order_ref),
        (rates_hbm, rates_ref),
        (u_hbm, u_ref),
        (k_hbm, k_ref),
    )
    copies = [pltpu.make_async_copy(src, dst, sems.at[n]) for n, (src, dst) in enumerate(pairs)]
    for copy in copies:
        copy.start()
    for copy in copies:
        copy.wait()
    here = here_ref[0]
    for side in range(2):
        beside = neighbours_ref[side, here]
        plan_ref[side] = jnp.bitwise_xor(jnp.maximum(beside, 0), here)
        plan_ref[2 + side] = (beside >= 0).astype(jnp.int32)
    order = [order_ref[r] for r in range(ROUNDS)]
    low = jnp.minimum(jnp.minimum(order[0], order[1]), order[2])
    high = order[0] + order[1] + order[2] - top - low
    branch_ref[0] = ((low * (2 * top - 1 - low)) >> 1) + high - low - 1

    def source(slot):
        for r in reversed(range(ROUNDS)):
            partner = jnp.bitwise_xor(slot, jnp.left_shift(jnp.int32(1), order[r]))
            slot = jnp.where(migrate_ref[r, slot] + migrate_ref[r, partner] > 0, partner, slot)
        return slot

    def candidate(slot):
        apart = jnp.bitwise_xor(source(slot), here)
        return ((apart >> top) & 1) + 2 * ((apart >> low) & 1), (apart >> high) & 1

    plan_ref[5], _ = candidate(jnp.bitwise_xor(here, jnp.left_shift(jnp.int32(1), high)))
    plan_ref[6], plan_ref[7] = candidate(here)
    depth = k_ref.shape[0]
    wide = lax.broadcasted_iota(jnp.int32, (LANES, LANES), 1)
    for a in range(3):
        packed = jnp.zeros((LANES, LANES), jnp.float32)
        for z in range(depth):
            plane = k_ref[z] if a == 2 else u_ref[a, z]
            moved = pltpu.roll(plane, (16 * z + 8) % LANES, 1)
            packed = jnp.where((wide >= 16 * z) & (wide < 16 * z + 16), moved, packed)
        turned = packed.T
        own_ref[a] = turned.reshape(depth, 16, LANES)
        for z in range(depth):
            high = turned[16 * z : 16 * z + 8]
            low = turned[16 * z + 8 : 16 * z + 16]
            sent_ref[a * depth + z] = pltpu.roll(jnp.where(row_index() < 4, low, high), 4, 0)
    for r in range(2):
        sent_ref[3 * depth + r] = jnp.full((ROWS, LANES), rates_ref[0, r], jnp.float32)


def interior_kernel(first, cuts, velocity_ref, rates_ref, u_ref, k_ref, *refs):
    out_refs, (ub, kp, kxr, kxl, ky, kz, c0) = refs[: len(cuts)], refs[len(cuts) :]
    depth, height, _ = k_ref.shape
    blocks = height // ROWS
    last = first + sum(cuts)
    start, stop = max(first - 1, 0), min(last + 1, blocks)
    half = 0.5 * time_step
    zero = jnp.zeros((ROWS, LANES), jnp.float32)
    low, high = max(start - 1, 0) * ROWS, min(stop + 1, blocks) * ROWS
    for z in range(depth):
        for edge in (0, height + ROWS):
            kp[z, edge : edge + ROWS] = zero
            ky[z, edge : edge + ROWS] = zero
            for s in range(2):
                for i in range(2):
                    ub[s, i, z, edge : edge + ROWS] = zero
        kp[z, ROWS + low : ROWS + high] = k_ref[z, low:high]
        for i in range(2):
            ub[0, i, z, ROWS + low : ROWS + high] = u_ref[i, z, low:high]
    pos = [[speeds(velocity_ref, i, d) for d in range(3)] for i in range(2)]
    decay = time_step * rates_ref[0, 1]
    growth = time_step * rates_ref[0, 0]

    def coefficients(b, _):
        y = pl.multiple_of(b * ROWS, ROWS)
        at = y + ROWS
        row = row_index() + y
        has_next = (row < height - 1).astype(jnp.float32)
        has_prior = (row > 0).astype(jnp.float32)
        below = zero
        for z in range(depth):
            k = kp[z, pl.ds(at, ROWS)]
            xr = half * (k + pltpu.roll(k, LANES - 1, 1))
            xl = pltpu.roll(xr, 1, 1)
            yr = half * (k + kp[z, pl.ds(at + 1, ROWS)]) * has_next
            yl = half * (k + kp[z, pl.ds(at - 1, ROWS)]) * has_prior
            above = half * (k + kp[z + 1, pl.ds(at, ROWS)]) if z < depth - 1 else zero
            kxr[z, pl.ds(y, ROWS)] = xr
            kxl[z, pl.ds(y, ROWS)] = xl
            ky[z, pl.ds(at, ROWS)] = yr
            kz[z, pl.ds(y, ROWS)] = above
            total = 1.0 - ((xr + xl) + (yr + yl) + (above + below))
            for i in range(2):
                (px, mx), (py, my), (pz, mz) = pos[i]
                level = px - mx
                if z < depth - 1:
                    level = level + pz
                if z > 0:
                    level = level - mz
                if i == 1:
                    level = level + decay
                c0[i, z, pl.ds(y, ROWS)] = total - (level + py * has_next - my * has_prior)
            below = above
        return 0

    lax.fori_loop(start, stop, coefficients, 0)

    def advance(src, put, b, _):
        y = pl.multiple_of(b * ROWS, ROWS)
        at = y + ROWS
        prior = [zero, zero]
        here = [ub[src, i, 0, pl.ds(at, ROWS)] for i in range(2)]
        zl = zero
        for z in range(depth):
            end = z == depth - 1
            after = [zero, zero] if end else [ub[src, i, z + 1, pl.ds(at, ROWS)] for i in range(2)]
            xr = kxr[z, pl.ds(y, ROWS)]
            xl = kxl[z, pl.ds(y, ROWS)]
            yr = ky[z, pl.ds(at, ROWS)]
            yl = ky[z, pl.ds(at - 1, ROWS)]
            zr = kz[z, pl.ds(y, ROWS)]
            q = (growth * here[0]) * here[1]
            for i in range(2):
                (px, mx), (py, my), (pz, mz) = pos[i]
                u = here[i]
                new = c0[i, z, pl.ds(y, ROWS)] * u
                new = new + (xr - mx) * pltpu.roll(u, LANES - 1, 1) + (xl + px) * pltpu.roll(u, 1, 1)
                new = new + (
                    (yr - my) * ub[src, i, z, pl.ds(at + 1, ROWS)] + (yl + py) * ub[src, i, z, pl.ds(at - 1, ROWS)]
                )
                if not end:
                    new = new + (zr - mz) * after[i]
                if z > 0:
                    new = new + (zl + pz) * prior[i]
                put(b, i, z, new - q if i == 0 else new + q)
            prior, here, zl = here, after, zr
        return 0

    for step in range(STEPS - 1):

        def keep(b, i, z, new, step=step):
            ub[1 - step % 2, i, z, pl.ds(pl.multiple_of(b * ROWS + ROWS, ROWS), ROWS)] = new

        lax.fori_loop(start, stop, partial(advance, step % 2, keep), 0)
    begin = first
    for cut, out_ref in zip(cuts, out_refs):

        def give(b, i, z, new, out_ref=out_ref, begin=begin):
            out_ref[i, z, pl.ds(pl.multiple_of((b - begin) * ROWS, ROWS), ROWS)] = new

        lax.fori_loop(begin, begin + cut, partial(advance, (STEPS - 1) % 2, give), 0)
        begin += cut


def edge_kernel(plan_ref, velocity_ref, rates_ref, left_ref, right_ref, own_ref, out_ref, ub, kp, kxr, kxl, ky, kz, c0):
    depth = own_ref.shape[1]
    half = 0.5 * time_step
    zero = jnp.zeros((ROWS, LANES), jnp.float32)
    row = row_index()
    lane = lane_index()
    kept = jnp.where(row < 4, plan_ref[3], plan_ref[2]).astype(jnp.float32)

    def beside(tile):
        both = jnp.where(row < 4, left_ref[0, tile], right_ref[0, tile])
        return pltpu.roll(both, 4, 0) * kept

    decay = [jnp.full((ROWS, LANES), time_step * rates_ref[0, 1])] * 3
    growth = [jnp.full((ROWS, LANES), time_step * rates_ref[0, 0])] * 3
    growth[1] = time_step * beside(3 * depth)
    decay[1] = time_step * beside(3 * depth + 1)
    pos = [[speeds(velocity_ref, i, d) for d in range(3)] for i in range(2)]
    has_next = (lane < LANES - 1).astype(jnp.float32)
    has_prior = (lane > 0).astype(jnp.float32)
    ends = [(pos[i][1][0] * has_prior, pos[i][1][1] * has_next) for i in range(2)]
    for z in range(depth + 2):
        inside = 0 < z < depth + 1
        for block in range(5):
            at = slice(block * ROWS, block * ROWS + ROWS)
            for s in range(2):
                for i in range(2):
                    if not inside or block in (0, 4):
                        ub[s, i, z, at] = zero
            if not inside or block in (0, 4):
                kp[z, at] = zero
        if inside:
            for a in range(3):
                parts = [own_ref[a, z - 1, 0:8], beside(a * depth + z - 1), own_ref[a, z - 1, 8:16]]
                for block in range(3):
                    at = slice(block * ROWS + ROWS, block * ROWS + 2 * ROWS)
                    if a == 2:
                        kp[z, at] = parts[block]
                    else:
                        ub[0, a, z, at] = parts[block]
    for block in range(3):
        kz[0, block * ROWS : block * ROWS + ROWS] = zero

    def coefficients(z, _):
        upper = (z < depth).astype(jnp.float32)
        lower = (z > 1).astype(jnp.float32)
        for block in range(3):
            at = ROWS * (block + 1)
            here = slice(at, at + ROWS)
            put = slice(block * ROWS, block * ROWS + ROWS)
            k = kp[z, here]
            xr = half * (k + kp[z, at + 1 : at + 1 + ROWS])
            xl = half * (k + kp[z, at - 1 : at - 1 + ROWS])
            yr = half * (k + pltpu.roll(k, LANES - 1, 1)) * has_next
            yl = pltpu.roll(yr, 1, 1)
            zr = half * upper * (k + kp[z + 1, here])
            zl = half * lower * (k + kp[z - 1, here])
            kxr[z, put] = xr
            kxl[z, put] = xl
            ky[z, put] = yr
            kz[z, put] = zr
            total = 1.0 - ((xr + xl) + (yr + yl) + (zr + zl))
            for i in range(2):
                (px, mx), (py, my), (pz, mz) = pos[i]
                level = px - mx + pz * upper - mz * lower + (py * has_next - my * has_prior)
                if i == 1:
                    level = level + decay[block]
                c0[i, z, put] = total - level
        return 0

    lax.fori_loop(1, depth + 1, coefficients, 0)

    for step in range(STEPS):
        src = step % 2

        def advance(z, _):
            for block in range(3):
                at = ROWS * (block + 1)
                here = slice(at, at + ROWS)
                put = slice(block * ROWS, block * ROWS + ROWS)
                xr, xl, yr, zr, zl = kxr[z, put], kxl[z, put], ky[z, put], kz[z, put], kz[z - 1, put]
                yl = pltpu.roll(yr, 1, 1)
                pair = [ub[src, i, z, here] for i in range(2)]
                q = (growth[block] * pair[0]) * pair[1]
                for i in range(2):
                    (px, mx), _, (pz, mz) = pos[i]
                    py, my = ends[i]
                    u = pair[i]
                    new = c0[i, z, put] * u
                    new = new + (xr - mx) * ub[src, i, z, at + 1 : at + 1 + ROWS]
                    new = new + (xl + px) * ub[src, i, z, at - 1 : at - 1 + ROWS]
                    new = new + ((yr - my) * pltpu.roll(u, LANES - 1, 1) + (yl + py) * pltpu.roll(u, 1, 1))
                    new = new + ((zr - mz) * ub[src, i, z + 1, here] + (zl + pz) * ub[src, i, z - 1, here])
                    new = new - q if i == 0 else new + q
                    if block == 1:
                        new = new * kept
                    ub[1 - src, i, z, here] = new
            return 0

        lax.fori_loop(1, depth + 1, advance, 0)
    for i in range(2):
        for z in range(depth):
            high = ub[STEPS % 2, i, z + 1, ROWS : 2 * ROWS]
            low = ub[STEPS % 2, i, z + 1, 3 * ROWS : 4 * ROWS]
            out_ref[i, z] = pltpu.roll(jnp.where(row < 4, low, high), 4, 0)


def merge_kernel(*refs):
    *part_refs, edge_ref, out_ref = refs
    depth = out_ref.shape[1]
    turned = edge_ref[...].reshape(2 * depth * ROWS, LANES).T
    begin = 0
    for part_ref in part_refs:
        rows = part_ref.shape[2]
        wide = lax.broadcasted_iota(jnp.int32, (rows, LANES), 1)
        rim = (wide < 4) | (wide >= LANES - 4)
        for i in range(2):
            for z in range(depth):
                shift = (LANES - 4 - ROWS * (i * depth + z)) % LANES
                turn = pltpu.roll(turned[begin : begin + rows], shift, 1)
                out_ref[i, z, begin : begin + rows] = jnp.where(rim, turn, part_ref[i, z])
        begin += rows


def swap_mask(block, mask):
    return lax.ppermute(block, AXES, [(slot, slot ^ mask) for slot in range(lax.axis_size(AXES))])


def swap(block, bit):
    return swap_mask(block, 1 << bit)


def swap_both(block, first, second):
    return swap_mask(block, 1 << first | 1 << second)


def pick(index, options):
    picked = options[0]
    for number in range(1, 4):
        picked = jnp.where(index == number, options[number], picked)
    return picked


def order(*values):
    return lax.optimization_barrier(values)


def interior_call(first, cuts, velocity, rates, field, kappa):
    species, depth, height, width = field.shape
    f32 = jnp.float32
    padded = height + 2 * ROWS
    return pl.pallas_call(
        partial(interior_kernel, first, cuts),
        out_shape=[jax.ShapeDtypeStruct((species, depth, cut * ROWS, width), f32) for cut in cuts],
        in_specs=[SMEM] * 2 + [VMEM] * 2,
        out_specs=[VMEM] * len(cuts),
        scratch_shapes=[
            pltpu.VMEM((2, species, depth, padded, width), f32),
            pltpu.VMEM((depth, padded, width), f32),
            pltpu.VMEM((depth, height, width), f32),
            pltpu.VMEM((depth, height, width), f32),
            pltpu.VMEM((depth, padded, width), f32),
            pltpu.VMEM((depth, height, width), f32),
            pltpu.VMEM((species, depth, height, width), f32),
        ],
        compiler_params=PARAMS,
        cost_estimate=pl.CostEstimate(flops=40_000_000, bytes_accessed=10_000_000, transcendentals=0),
        name="interior",
    )(velocity, rates, field, kappa)


def edge_call(plan, velocity, rates, gathered, own, bits):
    f32 = jnp.float32
    species = 2
    depth = own.shape[1]
    tiles = gathered.shape[1]

    def spot(apart):
        place = 0
        for n, bit in enumerate(bits):
            place = place | (((apart >> bit) & 1) << n)
        return place

    return pl.pallas_call(
        edge_kernel,
        out_shape=jax.ShapeDtypeStruct((species, depth, ROWS, LANES), f32),
        grid_spec=pltpu.PrefetchScalarGridSpec(
            num_scalar_prefetch=1,
            grid=(1,),
            in_specs=[
                SMEM,
                SMEM,
                pl.BlockSpec((1, tiles, ROWS, LANES), lambda i, plan: (spot(plan[0]), 0, 0, 0)),
                pl.BlockSpec((1, tiles, ROWS, LANES), lambda i, plan: (spot(plan[1]), 0, 0, 0)),
                VMEM,
            ],
            out_specs=pl.BlockSpec((species, depth, ROWS, LANES), lambda i, plan: (0, 0, 0, 0)),
            scratch_shapes=[
                pltpu.VMEM((2, species, depth + 2, 40, LANES), f32),
                pltpu.VMEM((depth + 2, 40, LANES), f32),
                pltpu.VMEM((depth + 2, 24, LANES), f32),
                pltpu.VMEM((depth + 2, 24, LANES), f32),
                pltpu.VMEM((depth + 2, 24, LANES), f32),
                pltpu.VMEM((depth + 2, 24, LANES), f32),
                pltpu.VMEM((species, depth + 2, 24, LANES), f32),
            ],
        ),
        compiler_params=PARAMS,
        cost_estimate=pl.CostEstimate(flops=40_000_000, bytes_accessed=20_000_000, transcendentals=0),
        name="edges",
    )(plan, velocity, rates, gathered, gathered, own)


def double(strips, bit):
    return jnp.concatenate([strips, swap(strips, bit)], axis=0)


def run(low, high, top, field, kappa, rates, velocity, plan, own, sent):
    blocks = field.shape[2] // ROWS
    cuts = (blocks // 4,) * 4
    middle = [bit for bit in reversed(range(1, top)) if bit != low]
    if low:
        middle.insert(0, low)
    give = partial(pick, plan[5])
    keep = partial(pick, plan[6])

    def result(options, other):
        return jnp.where(plan[7] > 0, other, keep(options))

    strips = double(sent[None], top)
    (p0,) = interior_call(0, cuts[:1], velocity, rates, field, kappa)
    p0, strips, field = order(p0, strips, field)
    n0, a0 = swap(p0, top), swap(p0, low)
    strips = double(strips, middle[0])
    p1, p2, p3 = interior_call(cuts[0], cuts[1:], velocity, rates, field, kappa)
    p1, p2, p3, n0, a0, strips = order(p1, p2, p3, n0, a0, strips)
    n1, a1, f0 = swap(p1, top), swap(p1, low), swap(n0, low)
    for bit in middle[1:]:
        strips = double(strips, bit)
    p2, n1, a1, f0, strips = order(p2, n1, a1, f0, strips)
    o0 = (p0, n0, a0, f0)
    n2, a2, f1, h0 = swap(p2, top), swap(p2, low), swap(n1, low), swap(give(o0), high)
    strips = double(strips, 0)
    p3, n2, a2, f1, h0, strips = order(p3, n2, a2, f1, h0, strips)
    o1 = (p1, n1, a1, f1)
    n3, a3, f2, h1 = swap(p3, top), swap(p3, low), swap(n2, low), swap(give(o1), high)
    edges = edge_call(plan, velocity, rates, strips, own, [top, *middle, 0])
    edges, h1, f2 = order(edges, h1, f2)
    oe = (edges, swap(edges, top), swap(edges, low), swap_both(edges, top, low))
    n3, a3, f2, h1, *oe = order(n3, a3, f2, h1, *oe)
    o2 = (p2, n2, a2, f2)
    f3, h2 = swap(n3, low), swap(give(o2), high)
    eh = swap(give(oe), high)
    f3, h2, eh = order(f3, h2, eh)
    o3 = (p3, n3, a3, f3)
    h3 = swap(give(o3), high)
    parts = [result(*pair) for pair in ((o0, h0), (o1, h1), (o2, h2), (o3, h3), (oe, eh))]
    return pl.pallas_call(
        merge_kernel,
        out_shape=jax.ShapeDtypeStruct(field.shape, jnp.float32),
        in_specs=[VMEM] * 5,
        out_specs=VMEM,
        compiler_params=PARAMS,
        name="merge",
    )(*parts)


def per_device(concentration, diffusivity, rates, velocity, neighbours, migrate, bit_order):
    top = lax.axis_size(AXES).bit_length() - 2
    field = concentration[0]
    kappa = diffusivity[0]
    depth = kappa.shape[0]
    here = lax.axis_index(AXES).astype(jnp.int32).reshape(1)
    branch, plan, own, sent = pl.pallas_call(
        partial(prepare_kernel, top),
        out_shape=(
            jax.ShapeDtypeStruct((1,), jnp.int32),
            jax.ShapeDtypeStruct((8,), jnp.int32),
            jax.ShapeDtypeStruct((3, depth, 16, LANES), jnp.float32),
            jax.ShapeDtypeStruct((3 * depth + 2, ROWS, LANES), jnp.float32),
        ),
        in_specs=[SMEM] + [pl.BlockSpec(memory_space=pl.ANY)] * 6,
        out_specs=(SMEM, SMEM, VMEM, VMEM),
        scratch_shapes=[
            pltpu.SMEM(neighbours.shape[::-1], jnp.int32),
            pltpu.SMEM(migrate.shape, jnp.int32),
            pltpu.SMEM(bit_order.shape, jnp.int32),
            pltpu.SMEM(rates.shape, jnp.float32),
            pltpu.VMEM(field.shape, jnp.float32),
            pltpu.VMEM(kappa.shape, jnp.float32),
            pltpu.SemaphoreType.DMA((6,)),
        ],
        compiler_params=pltpu.CompilerParams(vmem_limit_bytes=60 * 2**20),
        name="prepare",
    )(here, neighbours.T, migrate, bit_order, rates, field, kappa)
    branches = [partial(run, low, high, top) for low, high in combinations(range(top), 2)]
    final = lax.switch(branch[0], branches, field, kappa, rates, velocity, plan, own, sent)
    return final.reshape(concentration.shape)


def solution(mesh):
    spread = ("groups",) + AXES
    in_specs = (
        P(spread, None, None, None, None),
        P(spread, None, None, None),
        P(spread, None),
        P("groups", None),
        P("groups", None),
        P(None, "groups"),
        P("groups"),
    )
    out_specs = P(spread, None, None, None, None)
    return jax.shard_map(per_device, mesh=mesh, in_specs=in_specs, out_specs=out_specs, check_vma=False)
```
